128 devices in a mesh: rad: 8 (over z_lo, y), lat: 16 (over z_hi, x, core).
Axes of the slice: x: 4, y: 4, z: 4 (z_hi: 2, z_lo: 2; z = z_hi * 2 + z_lo), core: 2. Of those that a mesh axis runs over, the one named last changes fastest.
Arguments:
- physical: bfloat16 [256, 8, 256, 1536], P(None, None, 'rad', 'lat'), may hold values from -6 to 6
- pair_slot: int32 [128], replicated, may hold values from 0 to 127, each once
- legendre: bfloat16 [128, 1536, 1024], P('lat'), may hold values from -0.15625 to 0.15625
- spectral_state: bfloat16 [128, 8, 256, 1024], P('lat', None, None, 'rad'), may hold values from -6 to 6
- inverses: bfloat16 [4, 4, 256, 256], replicated, may hold values from -0.375 to 0.375
- block_index: int32 [128, 1024], P('lat', 'rad'), may hold values from 0 to 3
Outputs:
- new_state: bfloat16 [128, 8, 256, 1024], P('lat', None, None, 'rad')
The draws below stay inside these ranges and needn't reach their ends.
Inputs may be any that keep to these rules, and one draw needn't show every extreme that they name: `pair_slot`: each slot is taken by exactly one pair.
All inputs are finite; a program needn't handle non-finite values.
Results may differ from the reference program's by a relative error of at most 0.0053.
Values may be sent and summed in bfloat16 or wider, within the bound.
No kernel may reach another device: no remote copies, remote signals or barrier semaphores. Data moves between devices by JAX's collectives and lax.ppermute only.
A program may use at most 192 MiB of HBM per device.

```python
import jax
import jax.numpy as jnp
from jax import lax

NLAT = 1536
LDEG = 1024
NR = 256
POT = 4
NPAIR = 128
NINV = 4
MW = 256


def touch_ends(result, rng, smallest, top_value):
    longest = result.shape.index(max(result.shape))
    spots = []
    for shift in (0, 1):
        where = [jax.random.randint(jax.random.fold_in(rng, axis), (), 0, length) for axis, length in enumerate(result.shape)]
        where[longest] = (where[longest] + shift) % result.shape[longest]
        spots.append(tuple(where))
    return result.at[spots[0]].set(smallest).at[spots[1]].set(top_value)


def steps_of(stream_key, shape, shards, smallest, top_value):
    factor_of, own = 1.0, jax.random.fold_in(stream_key, 6)
    for axis_at, blocks in shards:
        heights = jnp.exp(jax.random.uniform(jax.random.fold_in(own, axis_at), (blocks,), jnp.float32, smallest / len(shards), top_value / len(shards)))
        factor_of = factor_of * jnp.repeat(heights, shape[axis_at] // blocks).reshape([-1 if axis == axis_at else 1 for axis in range(len(shape))])
    return factor_of


def centred(stream_key, shape, deviation, bound, split=(), kind=jnp.bfloat16):
    values = jax.random.normal(stream_key, shape, jnp.float32) * deviation
    if len(split) > 0:
        values = steps_of(stream_key, shape, split, -0.22, 0.18) * values
    return jnp.clip(values, min=-bound, max=bound).astype(kind)


def setup_inputs(seed: int = 0) -> dict:
    splits = jax.random.split(jax.random.key(seed), 7)
    physical = centred(splits[0], (MW, 2 * POT, NR, NLAT), 1.0, 6.0, ((2, 8), (3, 16)))
    pair_slot = jax.random.permutation(splits[1], NPAIR).astype(jnp.int32)
    legendre = centred(splits[2], (NPAIR, NLAT, LDEG), NLAT ** -0.5, 0.15625, ((0, 16),))
    spectral_state = centred(splits[3], (NPAIR, 2 * POT, NR, LDEG), 1.0, 6.0, ((0, 16), (3, 8)))
    inverses = centred(splits[4], (POT, NINV, NR, NR), NR ** -0.5, 0.375)
    block_index = touch_ends(jax.random.randint(splits[5], (NPAIR, LDEG), 0, NINV), jax.random.fold_in(splits[5], 1), 0, NINV - 1).astype(jnp.int32)
    return {"physical": physical, "pair_slot": pair_slot, "legendre": legendre, "spectral_state": spectral_state, "inverses": inverses, "block_index": block_index}


def reference(physical, pair_slot, legendre, spectral_state, inverses, block_index):
    slot_ids = jnp.arange(NPAIR, dtype=jnp.int32)
    matches = pair_slot[None, :] == slot_ids[:, None]
    owners = jnp.sum(jnp.where(matches, slot_ids[None, :], 0), axis=1).astype(jnp.int32)
    row_order = (2 * owners[:, None] + jnp.arange(2, dtype=jnp.int32)[None, :]).reshape(-1)
    ordered = jnp.take(physical, row_order, axis=0)
    lengths = (LDEG - (1 + owners * (LDEG // 2 // NPAIR))).astype(jnp.int32)
    grouped = ordered.reshape(NPAIR, 2, 2 * POT, NR, NLAT)
    column = jnp.arange(LDEG, dtype=jnp.int32)

    def transform_pair(items):
        pair_rows, tables, length = items
        low_part = jnp.dot(pair_rows[0].reshape(-1, NLAT), tables, preferred_element_type=jnp.float32)
        high_part = jnp.dot(pair_rows[1].reshape(-1, NLAT), tables, preferred_element_type=jnp.float32)
        chosen = jnp.where(column[None, :] < length, low_part, high_part)
        return chosen.reshape(2 * POT, NR, LDEG).astype(jnp.bfloat16)

    spectral = lax.map(transform_pair, (grouped, legendre, lengths))
    right_side = (spectral_state.astype(jnp.float32) + 0.5 * spectral.astype(jnp.float32)).astype(jnp.bfloat16)

    def settle(items):
        slot_side, slot_index = items
        results = []
        for potential in range(POT):
            pot_part = slot_side[2 * potential:2 * potential + 2].astype(jnp.float32)
            summed = jnp.zeros((2, NR, LDEG), jnp.float32)
            for group in range(NINV):
                masked = jnp.where((slot_index == group)[None, None, :], pot_part, jnp.float32(0.0))
                summed = summed + jnp.einsum('ab,cbj->caj', inverses[potential, group].astype(jnp.float32), masked)
            results.append(summed)
        return jnp.concatenate(results, axis=0).astype(jnp.bfloat16)

    return lax.map(settle, (right_side, block_index))
```

```python
import functools

import jax
import jax.numpy as jnp
from jax import lax
from jax.experimental import pallas as pl
from jax.experimental.pallas import tpu as pltpu
from jax.sharding import PartitionSpec as P

ZS, Y = 2, 4
CHUNKS = (2, 2, 2, 1, 1)
STEP = 16
BF16, F32 = jnp.bfloat16, jnp.float32


def prep_kernel(starts, key_ref, x_ref, *refs):
    outs, (pick, wide, tall) = refs[: len(starts)], refs[len(starts) :]
    rows, step, orders = x_ref.shape
    per_dev = sum(n for _, n in starts)

    @pl.when(pl.program_id(0) == 0)
    def _():
        at = 0
        for first, n in starts:
            count = 16 * n * 2
            i = lax.broadcasted_iota(jnp.int32, (count, orders), 0)
            dest, rest = i // (2 * n), i % (2 * n)
            target = dest * (2 * per_dev) + 2 * first + rest
            hit = key_ref[...] == target
            pick[at : at + count, :] = jnp.where(hit, 1.0, 0.0).astype(BF16)
            at += count

    for lane in range(2):
        cols = slice(lane * 128, (lane + 1) * 128)
        wide[lane] = x_ref[:, :, cols].astype(F32).reshape(rows * step, 128)

    def body(n, carry):
        one = [wide[lane, pl.ds(n, rows, stride=step), :].astype(BF16) for lane in range(2)]
        moved = lax.dot_general(
            pick[...],
            jnp.concatenate(one, axis=1),
            (((1,), (1,)), ((), ())),
            preferred_element_type=F32,
        )
        for lane in range(2):
            cols = slice(lane * 128, (lane + 1) * 128)
            tall[lane, pl.ds(n, orders, stride=step), :] = moved[:, cols]
        return carry

    lax.fori_loop(0, step, body, 0)
    at = 0
    for out, (_, n) in zip(outs, starts):
        count = 16 * n * 2
        for lane in range(2):
            cols = slice(lane * 128, (lane + 1) * 128)
            part = tall[lane, at * step : (at + count) * step, :].astype(BF16)
            out[:, :, :, :, cols] = part.reshape(out.shape[:4] + (128,))
        at += count


def prep(physical, pair_slot, starts):
    orders, chans, radii, lats = physical.shape
    rows = chans * radii
    x = jnp.transpose(physical, (1, 2, 3, 0)).reshape(rows, lats, orders)
    key = (2 * pair_slot[:, None] + jnp.arange(2, dtype=jnp.int32)[None, :]).reshape(1, orders)
    return pl.pallas_call(
        functools.partial(prep_kernel, starts),
        grid=(lats // STEP,),
        in_specs=[
            pl.BlockSpec((1, orders), lambda b: (0, 0)),
            pl.BlockSpec((rows, STEP, orders), lambda b: (0, b, 0)),
        ],
        out_specs=[
            pl.BlockSpec((16, n, 2, STEP, rows), lambda b: (0, 0, 0, b, 0)) for _, n in starts
        ],
        out_shape=[jax.ShapeDtypeStruct((16, n, 2, lats, rows), BF16) for _, n in starts],
        scratch_shapes=[
            pltpu.VMEM((orders, orders), BF16),
            pltpu.VMEM((2, rows * STEP, 128), F32),
            pltpu.VMEM((2, orders * STEP, 128), F32),
        ],
        compiler_params=pltpu.CompilerParams(vmem_limit_bytes=48 << 20),
        cost_estimate=pl.CostEstimate(
            flops=2 * rows * lats * orders * orders,
            bytes_accessed=4 * rows * lats * orders,
            transcendentals=0,
        ),
        name="prep",
    )(key, x)


def transform_kernel(meta_ref, got_ref, table_ref, *refs):
    outs, full = refs[:8], refs[8]
    slot = pl.program_id(0)
    half = table_ref.shape[2] // 2
    depth = table_ref.shape[1]
    rows = got_ref.shape[4]
    low_in = got_ref[:, 0, 0].reshape(depth, rows)
    high_in = got_ref[:, 0, 1].reshape(depth, rows)
    length = meta_ref[9 + slot]
    dims = (((0,), (0,)), ((), ()))
    left = table_ref[0, :, :half]
    right = table_ref[0, :, half:]
    full[:, :half] = lax.dot_general(low_in, left, dims, preferred_element_type=F32).astype(BF16)
    low = lax.dot_general(low_in, right, dims, preferred_element_type=F32)
    high = lax.dot_general(high_in, right, dims, preferred_element_type=F32)
    column = half + lax.broadcasted_iota(jnp.int32, low.shape, 1)
    full[:, half:] = jnp.where(column < length, low, high).astype(BF16)
    for k in range(8):
        at = pl.multiple_of(meta_ref[1 + k] * 128, 128)
        outs[k][0, 0] = full[:, pl.ds(at, 128)]


def transform(got, legendre, meta, first):
    srcs, count, _, lats, rows = got.shape
    degrees = legendre.shape[2]
    depth = srcs // 2 * lats
    shape = (2, count, rows, 128)
    return pl.pallas_call(
        transform_kernel,
        grid_spec=pltpu.PrefetchScalarGridSpec(
            num_scalar_prefetch=1,
            grid=(count, 2),
            in_specs=[
                pl.BlockSpec(
                    (srcs // 2, 1, 2, lats, rows), lambda s, t, m: (t ^ m[0], s, 0, 0, 0)
                ),
                pl.BlockSpec((1, depth, degrees), lambda s, t, m: (first + s, t ^ m[0], 0)),
            ],
            out_specs=[pl.BlockSpec((1, 1, rows, 128), lambda s, t, m: (t, s, 0, 0))] * 8,
            scratch_shapes=[pltpu.VMEM((rows, degrees), BF16)],
        ),
        out_shape=[jax.ShapeDtypeStruct(shape, BF16)] * 8,
        compiler_params=pltpu.CompilerParams(vmem_limit_bytes=48 << 20),
        cost_estimate=pl.CostEstimate(
            flops=3 * 2 * count * rows * depth * degrees,
            bytes_accessed=4 * count * (2 * depth * rows * 2 + depth * degrees + rows * degrees),
            transcendentals=0,
        ),
        name="transform",
    )(meta, got, legendre)


def settle_kernel(first, meta_ref, *refs):
    parts = refs[:8]
    state_ref, index_ref, inv_ref = refs[8:11]
    out_ref, side = refs[-2], refs[-1]
    zl, y = meta_ref[0], meta_ref[1]
    radii = 32
    for ky in range(Y):
        near, far = parts[ky], parts[Y + ky]
        y_from = lax.rem(y + (Y - ky), Y)
        for t in range(2):
            at = pl.multiple_of(((zl ^ t) * Y + y_from) * radii, radii)
            for c in range(8):
                rows = slice(c * radii, (c + 1) * radii)
                total = near[t, 0, rows, :].astype(F32) + far[1 - t, 0, rows, :].astype(F32)
                value = state_ref[0, c, pl.ds(at, radii), :].astype(F32) + 0.5 * total
                lanes = slice((c % 2) * 128, (c % 2) * 128 + 128)
                side[c // 2, pl.ds(at, radii), lanes] = value.astype(BF16)
    row = index_ref[pl.ds(first + pl.program_id(0), 1), :]
    row = jnp.concatenate([row, row], axis=1)
    for q in range(4):
        acc = None
        for g in range(4):
            one = jnp.dot(inv_ref[q, g], side[q], preferred_element_type=F32)
            acc = one if acc is None else jnp.where(row == g, one, acc)
        acc = acc.astype(BF16)
        out_ref[0, 2 * q] = acc[:, :128]
        out_ref[0, 2 * q + 1] = acc[:, 128:]


def settle(parts, state, inverses, index, meta, first, so_far):
    count = parts[0].shape[1]
    block = pl.BlockSpec((2, 1) + parts[0].shape[2:], lambda s, m: (0, s, 0, 0))
    operands = [meta, *parts, state, index, inverses]
    in_specs = [block] * 8 + [
        pl.BlockSpec((1,) + state.shape[1:], lambda s, m: (first + s, 0, 0, 0)),
        pl.BlockSpec(index.shape, lambda s, m: (0, 0)),
        pl.BlockSpec(inverses.shape, lambda s, m: (0, 0, 0, 0)),
    ]
    aliases = {}
    if so_far is not None:
        operands.append(so_far)
        in_specs.append(pl.BlockSpec(memory_space=pl.ANY))
        aliases = {len(operands) - 1: 0}
    return pl.pallas_call(
        functools.partial(settle_kernel, first),
        grid_spec=pltpu.PrefetchScalarGridSpec(
            num_scalar_prefetch=1,
            grid=(count,),
            in_specs=in_specs,
            out_specs=pl.BlockSpec((1,) + state.shape[1:], lambda s, m: (first + s, 0, 0, 0)),
            scratch_shapes=[pltpu.VMEM((4, 256, 256), BF16)],
        ),
        out_shape=jax.ShapeDtypeStruct(state.shape, BF16),
        input_output_aliases=aliases,
        compiler_params=pltpu.CompilerParams(vmem_limit_bytes=48 << 20),
        cost_estimate=pl.CostEstimate(
            flops=2 * count * 16 * 256 * 256 * 256,
            bytes_accessed=count * (2 << 20) + (2 << 20),
            transcendentals=0,
        ),
        name="settle",
    )(*operands)


def flip_groups():
    groups = []
    for y in range(Y):
        for zl in range(ZS):
            groups.append([((zl ^ (l // 8)) * Y + y) * 16 + l for l in range(16)])
    return groups


def rad_targets(kz, ky):
    return [(i, ((i // Y) ^ kz) * Y + (i % Y + ky) % Y) for i in range(ZS * Y)]


def on_device(physical, pair_slot, legendre, spectral_state, inverses, block_index):
    pair_count = pair_slot.shape[0]
    per_dev, _, degrees = legendre.shape
    starts, first = [], 0
    for n in CHUNKS:
        starts.append((first, n))
        first += n
    sends = prep(physical, pair_slot, tuple(starts))

    lat, rad = lax.axis_index("lat"), lax.axis_index("rad")
    zl, y = rad // Y, rad % Y
    slots = lat * per_dev + jnp.arange(per_dev, dtype=jnp.int32)
    matches = pair_slot[None, :] == slots[:, None]
    owners = jnp.sum(jnp.where(matches, jnp.arange(pair_count, dtype=jnp.int32), 0), axis=1)
    stride = degrees // 2 // pair_count
    lengths = degrees - (1 + owners * stride)
    hops = jnp.arange(8, dtype=jnp.int32)
    blocks = (zl ^ (hops // Y)) * Y + (y + hops) % Y
    place = jnp.stack([zl, y]).astype(jnp.int32)

    out = None
    for send, (first, n) in zip(sends, starts):
        got = lax.all_to_all(
            send, ("rad", "lat"), 0, 0, tiled=True, axis_index_groups=flip_groups()
        )
        meta = jnp.concatenate(
            [(lat // 8)[None], blocks, lengths[first : first + n]]
        ).astype(jnp.int32)
        parts = transform(got, legendre, meta, first)
        moved = [parts[0]] + [
            lax.ppermute(parts[k], "rad", rad_targets(k // Y, k % Y)) for k in range(1, 8)
        ]
        out = settle(moved, spectral_state, inverses, block_index, place, first, out)
    return out


def solution(mesh):
    in_specs = (
        P(None, None, "rad", "lat"),
        P(),
        P("lat", None, None),
        P("lat", None, None, "rad"),
        P(),
        P("lat", "rad"),
    )
    out_specs = P("lat", None, None, "rad")
    return jax.shard_map(
        on_device, mesh=mesh, in_specs=in_specs, out_specs=out_specs, check_vma=False
    )
```

```python
import functools

import jax
import jax.numpy as jnp
from jax import lax
from jax.experimental import pallas as pl
from jax.experimental.pallas import tpu as pltpu
from jax.sharding import PartitionSpec as P

ZS, Y = 2, 4
CHUNKS = (3, 2, 2, 1)
TIES = ((1, (0, 4, 5, 6, 7)), (2, (1, 2, 3)))
STEP = 16
BF16, F32 = jnp.bfloat16, jnp.float32


def prep_kernel(starts, per_dev, key_ref, x_ref, *refs):
    outs, (pick, swap, by_lat, by_order) = refs[: len(starts)], refs[len(starts) :]
    rows, _, orders = x_ref.shape

    @pl.when(pl.program_id(0) == 0)
    def _():
        at = 0
        for first, n in starts:
            count = 16 * n * 2
            i = lax.broadcasted_iota(jnp.int32, (count, orders), 0)
            rest, dest = i // 16, i % 16
            target = dest * (2 * per_dev) + 2 * first + rest
            hit = key_ref[...] == target
            pick[at : at + count, :] = jnp.where(hit, 1.0, 0.0).astype(BF16)
            at += count
        i = lax.broadcasted_iota(jnp.int32, (256, 256), 0)
        j = lax.broadcasted_iota(jnp.int32, (256, 256), 1)
        hit = (i // 16 == j % 16) & (i % 16 == j // 16)
        swap[...] = jnp.where(hit, 1.0, 0.0).astype(BF16)

    def to_lat(c, carry):
        at = pl.multiple_of(c * 16, 16)
        block = x_ref[pl.ds(at, 16), :, :].reshape(256, orders)
        moved = jnp.dot(swap[...], block, preferred_element_type=F32)
        by_lat[:, pl.ds(at, 16), :] = moved.astype(BF16).reshape(STEP, 16, orders)
        return carry

    lax.fori_loop(0, rows // 16, to_lat, 0, unroll=True)

    def to_order(n, carry):
        moved = lax.dot_general(
            pick[...], by_lat[n], (((1,), (1,)), ((), ())), preferred_element_type=F32
        )
        by_order[:, n] = moved.astype(BF16).reshape(by_order.shape[0], 16, rows)
        return carry

    lax.fori_loop(0, STEP, to_order, 0, unroll=True)

    base = 0
    for out, (_, n) in zip(outs, starts):
        for g in range(2 * n):
            block = by_order[base + g].reshape(256, rows)
            moved = jnp.dot(swap[...], block, preferred_element_type=F32).astype(BF16)
            out[:, g // 2, g % 2] = moved.reshape(16, STEP, rows)
        base += 2 * n


def prep(physical, pair_slot, starts, per_dev):
    orders, chans, radii, lats = physical.shape
    sent = sum(32 * n for _, n in starts)
    rows = chans * radii
    x = jnp.transpose(physical, (1, 2, 3, 0)).reshape(rows, lats, orders)
    key = (2 * pair_slot[:, None] + jnp.arange(2, dtype=jnp.int32)[None, :]).reshape(1, orders)
    return pl.pallas_call(
        functools.partial(prep_kernel, starts, per_dev),
        grid=(lats // STEP,),
        in_specs=[
            pl.BlockSpec((1, orders), lambda b: (0, 0)),
            pl.BlockSpec((rows, STEP, orders), lambda b: (0, b, 0)),
        ],
        out_specs=[
            pl.BlockSpec((16, n, 2, STEP, rows), lambda b: (0, 0, 0, b, 0)) for _, n in starts
        ],
        out_shape=[jax.ShapeDtypeStruct((16, n, 2, lats, rows), BF16) for _, n in starts],
        scratch_shapes=[
            pltpu.VMEM((sent, orders), BF16),
            pltpu.VMEM((256, 256), BF16),
            pltpu.VMEM((STEP, rows, orders), BF16),
            pltpu.VMEM((sent // 16, STEP, 16, rows), BF16),
        ],
        compiler_params=pltpu.CompilerParams(vmem_limit_bytes=48 << 20),
        cost_estimate=pl.CostEstimate(
            flops=2 * rows * lats * orders * (orders + 2 * sent),
            bytes_accessed=2 * rows * lats * (orders + sent),
            transcendentals=0,
        ),
        name="prep",
    )(key, x)


def transform_kernel(meta_ref, got_ref, table_ref, *refs):
    outs, full = refs[:8], refs[8]
    slot = pl.program_id(0)
    half = table_ref.shape[2] // 2
    depth = table_ref.shape[1]
    rows = got_ref.shape[4]
    low_in = got_ref[:, 0, 0].reshape(depth, rows)
    high_in = got_ref[:, 0, 1].reshape(depth, rows)
    length = meta_ref[9 + slot]
    dims = (((0,), (0,)), ((), ()))
    left = table_ref[0, :, :half]
    right = table_ref[0, :, half:]
    full[:, :half] = lax.dot_general(low_in, left, dims, preferred_element_type=F32).astype(BF16)
    low = lax.dot_general(low_in, right, dims, preferred_element_type=F32)
    high = lax.dot_general(high_in, right, dims, preferred_element_type=F32)
    column = half + lax.broadcasted_iota(jnp.int32, low.shape, 1)
    full[:, half:] = jnp.where(column < length, low, high).astype(BF16)
    for k in range(8):
        at = pl.multiple_of(meta_ref[1 + k] * 128, 128)
        outs[k][0, 0] = full[:, pl.ds(at, 128)]


def transform(got, legendre, meta, first):
    srcs, count, _, lats, rows = got.shape
    degrees = legendre.shape[2]
    depth = srcs // 2 * lats
    shape = (2, count, rows, 128)
    return pl.pallas_call(
        transform_kernel,
        grid_spec=pltpu.PrefetchScalarGridSpec(
            num_scalar_prefetch=1,
            grid=(count, 2),
            in_specs=[
                pl.BlockSpec(
                    (srcs // 2, 1, 2, lats, rows), lambda s, t, m: (t ^ m[0], s, 0, 0, 0)
                ),
                pl.BlockSpec((1, depth, degrees), lambda s, t, m: (first + s, t ^ m[0], 0)),
            ],
            out_specs=[pl.BlockSpec((1, 1, rows, 128), lambda s, t, m: (t, s, 0, 0))] * 8,
            scratch_shapes=[pltpu.VMEM((rows, degrees), BF16)],
        ),
        out_shape=[jax.ShapeDtypeStruct(shape, BF16)] * 8,
        compiler_params=pltpu.CompilerParams(vmem_limit_bytes=48 << 20),
        cost_estimate=pl.CostEstimate(
            flops=3 * 2 * count * rows * depth * degrees,
            bytes_accessed=4 * count * (2 * depth * rows * 2 + depth * degrees + rows * degrees),
            transcendentals=0,
        ),
        name="transform",
    )(meta, got, legendre)


def transform_whole_kernel(meta_ref, got_ref, table_ref, out_ref):
    slot, part = pl.program_id(0), pl.program_id(1)
    srcs, _, _, lats, rows = got_ref.shape
    depth, width = srcs * lats, table_ref.shape[2]
    dims = (((0,), (0,)), ((), ()))

    def product(h):
        return lax.dot_general(
            got_ref[:, 0, h].reshape(depth, rows),
            table_ref[0],
            dims,
            preferred_element_type=F32,
        )

    def store(value):
        for d in range(width // 128):
            out_ref[d, 0] = value[:, d * 128 : (d + 1) * 128].astype(BF16)

    @pl.when(part == 0)
    def _():
        store(product(0))

    @pl.when(part == 1)
    def _():
        column = width + lax.broadcasted_iota(jnp.int32, (rows, width), 1)
        store(jnp.where(column < meta_ref[9 + slot], product(0), product(1)))


def transform_whole(got, legendre, meta, first):
    srcs, count, _, lats, rows = got.shape
    degrees = legendre.shape[2]
    depth = srcs * lats
    return pl.pallas_call(
        transform_whole_kernel,
        grid_spec=pltpu.PrefetchScalarGridSpec(
            num_scalar_prefetch=1,
            grid=(count, 2),
            in_specs=[
                pl.BlockSpec((srcs, 1, 2, lats, rows), lambda s, t, m: (0, s, 0, 0, 0)),
                pl.BlockSpec((1, depth, degrees // 2), lambda s, t, m: (first + s, 0, t)),
            ],
            out_specs=pl.BlockSpec((4, 1, rows, 128), lambda s, t, m: (t, s, 0, 0)),
        ),
        out_shape=jax.ShapeDtypeStruct((8, count, rows, 128), BF16),
        compiler_params=pltpu.CompilerParams(vmem_limit_bytes=48 << 20),
        cost_estimate=pl.CostEstimate(
            flops=3 * count * rows * depth * degrees,
            bytes_accessed=2 * count * (2 * depth * rows + depth * degrees + rows * degrees),
            transcendentals=0,
        ),
        name="transform_whole",
    )(meta, got, legendre)


def invert(row, inv_ref, out_ref, side):
    row = jnp.concatenate([row, row], axis=1)
    for q in range(4):
        acc = None
        for g in range(4):
            one = jnp.dot(inv_ref[q, g], side[q], preferred_element_type=F32)
            acc = one if acc is None else jnp.where(row == g, one, acc)
        acc = acc.astype(BF16)
        out_ref[0, 2 * q] = acc[:, :128]
        out_ref[0, 2 * q + 1] = acc[:, 128:]


def settle_kernel(first, meta_ref, *refs):
    parts = refs[:8]
    state_ref, index_ref, inv_ref = refs[8:11]
    out_ref, side = refs[-2], refs[-1]
    zl, y = meta_ref[0], meta_ref[1]
    radii = 32
    for ky in range(Y):
        near, far = parts[ky], parts[Y + ky]
        y_from = lax.rem(y + (Y - ky), Y)
        for t in range(2):
            at = pl.multiple_of(((zl ^ t) * Y + y_from) * radii, radii)
            for c in range(8):
                rows = slice(c * radii, (c + 1) * radii)
                total = near[t, 0, rows, :].astype(F32) + far[1 - t, 0, rows, :].astype(F32)
                value = state_ref[0, c, pl.ds(at, radii), :].astype(F32) + 0.5 * total
                lanes = slice((c % 2) * 128, (c % 2) * 128 + 128)
                side[c // 2, pl.ds(at, radii), lanes] = value.astype(BF16)
    invert(index_ref[pl.ds(first + pl.program_id(0), 1), :], inv_ref, out_ref, side)


def settle_whole_kernel(first, meta_ref, *refs):
    part, state_ref, index_ref, inv_ref = refs[:4]
    out_ref, side = refs[-2], refs[-1]
    radii = 32
    for c in range(8):
        lanes = slice((c % 2) * 128, (c % 2) * 128 + 128)
        for d in range(8):
            total = part[d, 0, c * radii : (c + 1) * radii, :].astype(F32)
            at = slice(d * radii, (d + 1) * radii)
            value = state_ref[0, c, at, :].astype(F32) + 0.5 * total
            side[c // 2, at, lanes] = value.astype(BF16)
    invert(index_ref[pl.ds(first + pl.program_id(0), 1), :], inv_ref, out_ref, side)


def settle(kernel, parts, state, inverses, index, meta, first, so_far):
    count = parts[0].shape[1]
    block = pl.BlockSpec(
        (parts[0].shape[0], 1) + parts[0].shape[2:], lambda s, m: (0, s, 0, 0)
    )
    operands = [meta, *parts, state, index, inverses]
    in_specs = [block] * len(parts) + [
        pl.BlockSpec((1,) + state.shape[1:], lambda s, m: (first + s, 0, 0, 0)),
        pl.BlockSpec(index.shape, lambda s, m: (0, 0)),
        pl.BlockSpec(inverses.shape, lambda s, m: (0, 0, 0, 0)),
    ]
    aliases = {}
    if so_far is not None:
        operands.append(so_far)
        in_specs.append(pl.BlockSpec(memory_space=pl.ANY))
        aliases = {len(operands) - 1: 0}
    return pl.pallas_call(
        functools.partial(kernel, first),
        grid_spec=pltpu.PrefetchScalarGridSpec(
            num_scalar_prefetch=1,
            grid=(count,),
            in_specs=in_specs,
            out_specs=pl.BlockSpec((1,) + state.shape[1:], lambda s, m: (first + s, 0, 0, 0)),
            scratch_shapes=[pltpu.VMEM((4, 256, 256), BF16)],
        ),
        out_shape=jax.ShapeDtypeStruct(state.shape, BF16),
        input_output_aliases=aliases,
        compiler_params=pltpu.CompilerParams(vmem_limit_bytes=48 << 20),
        cost_estimate=pl.CostEstimate(
            flops=2 * count * 16 * 256 * 256 * 256,
            bytes_accessed=count * (2 << 20) + (2 << 20),
            transcendentals=0,
        ),
        name="settle",
    )(*operands)


def flip_groups():
    groups = []
    for y in range(Y):
        for zl in range(ZS):
            groups.append([((zl ^ (l // 8)) * Y + y) * 16 + l for l in range(16)])
    return groups


def rad_targets(kz, ky):
    return [(i, ((i // Y) ^ kz) * Y + (i % Y + ky) % Y) for i in range(ZS * Y)]


def on_device(physical, pair_slot, legendre, spectral_state, inverses, block_index):
    pair_count = pair_slot.shape[0]
    per_dev, _, degrees = legendre.shape
    starts, first = [], 0
    for n in CHUNKS:
        starts.append((first, n))
        first += n
    sends = list(prep(physical, pair_slot, tuple(starts[:1]), per_dev))

    lat, rad = lax.axis_index("lat"), lax.axis_index("rad")
    zl, y = rad // Y, rad % Y
    slots = lat * per_dev + jnp.arange(per_dev, dtype=jnp.int32)
    matches = pair_slot[None, :] == slots[:, None]
    owners = jnp.sum(jnp.where(matches, jnp.arange(pair_count, dtype=jnp.int32), 0), axis=1)
    stride = degrees // 2 // pair_count
    lengths = degrees - (1 + owners * stride)
    hops = jnp.arange(8, dtype=jnp.int32)
    blocks = (zl ^ (hops // Y)) * Y + (y + hops) % Y
    place = jnp.stack([zl, y]).astype(jnp.int32)

    out, gots, moves = None, [], []

    final = len(starts) - 1

    def put(k):
        kernel = settle_whole_kernel if k == final else settle_kernel
        return settle(
            kernel, moves[k], spectral_state, inverses, block_index, place, starts[k][0], out
        )

    for k in range(len(starts) + 1):
        keep = {}
        if k > 0:
            keep["got", k - 1] = gots[k - 1]
        for back, hops_of in TIES:
            if k > back:
                for h in hops_of:
                    keep["move", k - 1 - back, h] = moves[k - 1 - back][h]
        if k > 2:
            keep["out"] = out
        if k < len(starts):
            if k == 1:
                sends.extend(prep(physical, pair_slot, tuple(starts[1:]), per_dev))
            keep["send", k] = sends[k]
        held = dict(zip(keep, lax.optimization_barrier(tuple(keep.values()))))
        out = held.get("out", out)
        if k > 0:
            gots[k - 1] = held["got", k - 1]
        for name, value in held.items():
            if name[0] == "move":
                moves[name[1]][name[2]] = value
        if k < len(starts):
            send = held["send", k]
            if k == final:
                gots.append(lax.all_to_all(send, "lat", 0, 0, tiled=True))
            else:
                gots.append(
                    lax.all_to_all(
                        send, ("rad", "lat"), 0, 0, tiled=True, axis_index_groups=flip_groups()
                    )
                )
        if k > 0:
            first, n = starts[k - 1]
            meta = jnp.concatenate([(lat // 8)[None], blocks, lengths[first : first + n]])
            meta = meta.astype(jnp.int32)
            if k - 1 == final:
                part = transform_whole(gots[k - 1], legendre, meta, first)
                moves.append([lax.all_to_all(part, "rad", 0, 0, tiled=True)])
            else:
                parts = transform(gots[k - 1], legendre, meta, first)
                moves.append(
                    [parts[0]]
                    + [
                        lax.ppermute(parts[h], "rad", rad_targets(h // Y, h % Y))
                        for h in range(1, 8)
                    ]
                )
        if k > 1:
            out = put(k - 2)
    return put(final)


def solution(mesh):
    in_specs = (
        P(None, None, "rad", "lat"),
        P(),
        P("lat", None, None),
        P("lat", None, None, "rad"),
        P(),
        P("lat", "rad"),
    )
    out_specs = P("lat", None, None, "rad")
    return jax.shard_map(
        on_device, mesh=mesh, in_specs=in_specs, out_specs=out_specs, check_vma=False
    )
```

```python
import functools

import jax
import jax.numpy as jnp
from jax import lax
from jax.experimental import pallas as pl
from jax.experimental.pallas import tpu as pltpu
from jax.sharding import PartitionSpec as P

ZS, Y = 2, 4
CHUNKS = (4, 2, 2)
FLIPPED = (False, True, True)
TIES = {2: ((0, (0, 1, 2, 3, 4, 5)),), 3: ((0, (6, 7)), (1, range(8)))}
STEP = 16
BF16, F32 = jnp.bfloat16, jnp.float32


def prep_kernel(starts, per_dev, key_ref, x_ref, *refs):
    outs, (pick, swap, by_lat, by_order) = refs[: len(starts)], refs[len(starts) :]
    rows, _, orders = x_ref.shape

    @pl.when(pl.program_id(0) == 0)
    def _():
        at = 0
        for first, n in starts:
            count = 16 * n * 2
            i = lax.broadcasted_iota(jnp.int32, (count, orders), 0)
            rest, dest = i // 16, i % 16
            target = dest * (2 * per_dev) + 2 * first + rest
            hit = key_ref[...] == target
            pick[at : at + count, :] = jnp.where(hit, 1.0, 0.0).astype(BF16)
            at += count
        i = lax.broadcasted_iota(jnp.int32, (256, 256), 0)
        j = lax.broadcasted_iota(jnp.int32, (256, 256), 1)
        hit = (i // 16 == j % 16) & (i % 16 == j // 16)
        swap[...] = jnp.where(hit, 1.0, 0.0).astype(BF16)

    def to_lat(c, carry):
        at = pl.multiple_of(c * 16, 16)
        block = x_ref[pl.ds(at, 16), :, :].reshape(256, orders)
        moved = jnp.dot(swap[...], block, preferred_element_type=F32)
        by_lat[:, pl.ds(at, 16), :] = moved.astype(BF16).reshape(STEP, 16, orders)
        return carry

    lax.fori_loop(0, rows // 16, to_lat, 0, unroll=True)

    def to_order(n, carry):
        moved = lax.dot_general(
            pick[...], by_lat[n], (((1,), (1,)), ((), ())), preferred_element_type=F32
        )
        by_order[:, n] = moved.astype(BF16).reshape(by_order.shape[0], 16, rows)
        return carry

    lax.fori_loop(0, STEP, to_order, 0, unroll=True)

    base = 0
    for out, (_, n) in zip(outs, starts):
        for g in range(2 * n):
            block = by_order[base + g].reshape(256, rows)
            moved = jnp.dot(swap[...], block, preferred_element_type=F32).astype(BF16)
            out[:, g // 2, g % 2] = moved.reshape(16, STEP, rows)
        base += 2 * n


def prep(physical, pair_slot, starts, per_dev):
    orders, chans, radii, lats = physical.shape
    sent = sum(32 * n for _, n in starts)
    rows = chans * radii
    x = jnp.transpose(physical, (1, 2, 3, 0)).reshape(rows, lats, orders)
    key = (2 * pair_slot[:, None] + jnp.arange(2, dtype=jnp.int32)[None, :]).reshape(1, orders)
    return pl.pallas_call(
        functools.partial(prep_kernel, starts, per_dev),
        grid=(lats // STEP,),
        in_specs=[
            pl.BlockSpec((1, orders), lambda b: (0, 0)),
            pl.BlockSpec((rows, STEP, orders), lambda b: (0, b, 0)),
        ],
        out_specs=[
            pl.BlockSpec((16, n, 2, STEP, rows), lambda b: (0, 0, 0, b, 0)) for _, n in starts
        ],
        out_shape=[pltpu.HBM((16, n, 2, lats, rows), BF16) for _, n in starts],
        scratch_shapes=[
            pltpu.VMEM((sent, orders), BF16),
            pltpu.VMEM((256, 256), BF16),
            pltpu.VMEM((STEP, rows, orders), BF16),
            pltpu.VMEM((sent // 16, STEP, 16, rows), BF16),
        ],
        compiler_params=pltpu.CompilerParams(vmem_limit_bytes=48 << 20),
        cost_estimate=pl.CostEstimate(
            flops=2 * rows * lats * orders * (orders + 2 * sent),
            bytes_accessed=2 * rows * lats * (orders + sent),
            transcendentals=0,
        ),
        name="prep",
    )(key, x)


def spread(full, row, meta_ref, outs):
    for k in range(8):
        if len(outs) == 8:
            at = pl.multiple_of(meta_ref[1 + k] * 128, 128)
            outs[k][row] = full[:, pl.ds(at, 128)]
        else:
            outs[0][(k, *row)] = full[:, k * 128 : (k + 1) * 128]


def transform_kernel(meta_ref, got_ref, table_ref, *refs):
    outs, full = refs[:-1], refs[-1]
    slot = pl.program_id(0)
    half = table_ref.shape[2] // 2
    depth = table_ref.shape[1]
    rows = got_ref.shape[4]
    low_in = got_ref[:, 0, 0].reshape(depth, rows)
    high_in = got_ref[:, 0, 1].reshape(depth, rows)
    length = meta_ref[9 + slot]
    dims = (((0,), (0,)), ((), ()))
    low = lax.dot_general(low_in, table_ref[0], dims, preferred_element_type=F32)
    high = lax.dot_general(high_in, table_ref[0, :, half:], dims, preferred_element_type=F32)
    column = half + lax.broadcasted_iota(jnp.int32, high.shape, 1)
    full[:, :half] = low[:, :half].astype(BF16)
    full[:, half:] = jnp.where(column < length, low[:, half:], high).astype(BF16)
    spread(full, (0, 0), meta_ref, outs)


def transform_whole_kernel(meta_ref, got_ref, table_ref, *refs):
    outs, full = refs[:-1], refs[-1]
    slot, part = pl.program_id(0), pl.program_id(1)
    srcs, _, _, lats, rows = got_ref.shape
    depth, width = srcs * lats, table_ref.shape[2]
    dims = (((0,), (0,)), ((), ()))

    def product(h):
        return lax.dot_general(
            got_ref[:, 0, h].reshape(depth, rows),
            table_ref[0],
            dims,
            preferred_element_type=F32,
        )

    @pl.when(part == 0)
    def _():
        full[:, :width] = product(0).astype(BF16)

    @pl.when(part == 1)
    def _():
        column = width + lax.broadcasted_iota(jnp.int32, (rows, width), 1)
        chosen = jnp.where(column < meta_ref[9 + slot], product(0), product(1))
        full[:, width:] = chosen.astype(BF16)
        spread(full, (0,), meta_ref, outs)


def transform(got, legendre, meta, first, flipped, by_hop):
    srcs, count, _, lats, rows = got.shape
    degrees = legendre.shape[2]
    if flipped:
        kernel = transform_kernel
        depth, width = srcs // 2 * lats, degrees
        got_spec = pl.BlockSpec(
            (srcs // 2, 1, 2, lats, rows), lambda s, t, m: (t ^ m[0], s, 0, 0, 0)
        )
        table_spec = pl.BlockSpec((1, depth, width), lambda s, t, m: (first + s, t ^ m[0], 0))
        shape, block = (2, count, rows, 128), (1, 1, rows, 128)
        where = lambda s, t, m: (t, s, 0, 0)
    else:
        kernel = transform_whole_kernel
        depth, width = srcs * lats, degrees // 2
        got_spec = pl.BlockSpec((srcs, 1, 2, lats, rows), lambda s, t, m: (0, s, 0, 0, 0))
        table_spec = pl.BlockSpec((1, depth, width), lambda s, t, m: (first + s, 0, t))
        shape, block = (count, rows, 128), (1, rows, 128)
        where = lambda s, t, m: (s, 0, 0)
    if by_hop:
        out_specs = [pl.BlockSpec(block, where)] * 8
        out_shape = [pltpu.HBM(shape, BF16)] * 8
    else:
        out_specs = pl.BlockSpec((8,) + block, lambda s, t, m: (0, *where(s, t, m)))
        out_shape = pltpu.HBM((8,) + shape, BF16)
    return pl.pallas_call(
        kernel,
        grid_spec=pltpu.PrefetchScalarGridSpec(
            num_scalar_prefetch=1,
            grid=(count, 2),
            in_specs=[got_spec, table_spec],
            out_specs=out_specs,
            scratch_shapes=[pltpu.VMEM((rows, degrees), BF16)],
        ),
        out_shape=out_shape,
        compiler_params=pltpu.CompilerParams(vmem_limit_bytes=48 << 20),
        cost_estimate=pl.CostEstimate(
            flops=3 * count * rows * srcs * lats * degrees,
            bytes_accessed=2 * count * srcs * lats * (2 * rows + degrees),
            transcendentals=0,
        ),
        name="transform",
    )(meta, got, legendre)


def invert(row, inv_ref, out_ref, side):
    row = jnp.concatenate([row, row], axis=1)
    for q in range(4):
        every = inv_ref[q].reshape(4 * 256, 256)
        found = jnp.dot(every, side[q], preferred_element_type=F32)
        acc = found[:256]
        for g in range(1, 4):
            acc = jnp.where(row == g, found[g * 256 : (g + 1) * 256], acc)
        acc = acc.astype(BF16)
        out_ref[0, 2 * q] = acc[:, :128]
        out_ref[0, 2 * q + 1] = acc[:, 128:]


def settle_kernel(first, flipped, meta_ref, *refs):
    parts = refs[:-5]
    state_ref, index_ref, inv_ref, out_ref, side = refs[-5:]
    radii = 32

    def part(zs, ys, *where):
        if len(parts) == 8:
            return parts[zs * Y + ys][where].astype(F32)
        return parts[0][(zs * Y + ys, *where)].astype(F32)

    for zs in range(ZS):
        for ys in range(Y):
            at = (zs * Y + ys) * radii
            if len(parts) == 8:
                zl, y = meta_ref[0], meta_ref[1]
                at = pl.multiple_of(((zl ^ zs) * Y + lax.rem(y + (Y - ys), Y)) * radii, radii)
            for c in range(8):
                rows = slice(c * radii, (c + 1) * radii)
                if flipped:
                    total = part(zs, ys, 0, 0, rows) + part(1 - zs, ys, 1, 0, rows)
                else:
                    total = part(zs, ys, 0, rows)
                value = state_ref[0, c, pl.ds(at, radii), :].astype(F32) + 0.5 * total
                lanes = slice((c % 2) * 128, (c % 2) * 128 + 128)
                side[c // 2, pl.ds(at, radii), lanes] = value.astype(BF16)
    invert(index_ref[pl.ds(first + pl.program_id(0), 1), :], inv_ref, out_ref, side)


def settle_chained_kernel(first, flipped, meta_ref, *refs):
    settle_kernel(first, flipped, meta_ref, *refs[:-3], *refs[-2:])


def settle(parts, state, inverses, index, meta, first, count, flipped, so_far):
    shape = parts[0].shape
    block = [1 if i == len(shape) - 3 else n for i, n in enumerate(shape)]
    lead = (0,) * (len(shape) - 3)
    operands = [meta, *parts, state, index, inverses]
    in_specs = [pl.BlockSpec(block, lambda s, m: (*lead, s, 0, 0))] * len(parts) + [
        pl.BlockSpec((1,) + state.shape[1:], lambda s, m: (first + s, 0, 0, 0)),
        pl.BlockSpec(index.shape, lambda s, m: (0, 0)),
        pl.BlockSpec(inverses.shape, lambda s, m: (0, 0, 0, 0)),
    ]
    kernel = settle_kernel if so_far is None else settle_chained_kernel
    aliases = {}
    if so_far is not None:
        operands.append(so_far)
        in_specs.append(pl.BlockSpec(memory_space=pl.ANY))
        aliases = {len(operands) - 1: 0}
    return pl.pallas_call(
        functools.partial(kernel, first, flipped),
        grid_spec=pltpu.PrefetchScalarGridSpec(
            num_scalar_prefetch=1,
            grid=(count,),
            in_specs=in_specs,
            out_specs=pl.BlockSpec((1,) + state.shape[1:], lambda s, m: (first + s, 0, 0, 0)),
            scratch_shapes=[pltpu.VMEM((4, 256, 256), BF16)],
        ),
        out_shape=jax.ShapeDtypeStruct(state.shape, BF16),
        input_output_aliases=aliases,
        compiler_params=pltpu.CompilerParams(vmem_limit_bytes=48 << 20),
        cost_estimate=pl.CostEstimate(
            flops=2 * count * 16 * 256 * 256 * 256,
            bytes_accessed=count * (2 << 20) + (2 << 20),
            transcendentals=0,
        ),
        name="settle",
    )(*operands)


def flip_groups():
    groups = []
    for y in range(Y):
        for zl in range(ZS):
            groups.append([((zl ^ (l // 8)) * Y + y) * 16 + l for l in range(16)])
    return groups


def rad_targets(kz, ky):
    return [(i, ((i // Y) ^ kz) * Y + (i % Y + ky) % Y) for i in range(ZS * Y)]


def on_device(physical, pair_slot, legendre, spectral_state, inverses, block_index):
    pair_count = pair_slot.shape[0]
    per_dev, _, degrees = legendre.shape
    starts, first = [], 0
    for n in CHUNKS:
        starts.append((first, n))
        first += n
    sends = list(prep(physical, pair_slot, tuple(starts[:1]), per_dev))

    lat, rad = lax.axis_index("lat"), lax.axis_index("rad")
    zl, y = rad // Y, rad % Y
    slots = lat * per_dev + jnp.arange(per_dev, dtype=jnp.int32)
    matches = pair_slot[None, :] == slots[:, None]
    owners = jnp.sum(jnp.where(matches, jnp.arange(pair_count, dtype=jnp.int32), 0), axis=1)
    stride = degrees // 2 // pair_count
    lengths = degrees - (1 + owners * stride)
    hops = jnp.arange(8, dtype=jnp.int32)
    blocks = (zl ^ (hops // Y)) * Y + (y + hops) % Y
    place = jnp.stack([zl, y]).astype(jnp.int32)

    out, gots, moves = None, [], []

    final = len(starts) - 1

    def put(k):
        return settle(
            moves[k],
            spectral_state,
            inverses,
            block_index,
            place,
            *starts[k],
            FLIPPED[k],
            out,
        )

    for k in range(len(starts) + 1):
        keep = {}
        if k > 0:
            keep["got", k - 1] = gots[k - 1]
        for chunk, hops_of in TIES.get(k, ()):
            for h in hops_of:
                keep["move", chunk, h] = moves[chunk][h]
        if k > 2:
            keep["out"] = out
        if k < len(starts):
            if k == 1:
                sends.extend(prep(physical, pair_slot, tuple(starts[1:]), per_dev))
            keep["send", k] = sends[k]
        held = dict(zip(keep, lax.optimization_barrier(tuple(keep.values()))))
        out = held.get("out", out)
        if k > 0:
            gots[k - 1] = held["got", k - 1]
        for name, value in held.items():
            if name[0] == "move":
                moves[name[1]][name[2]] = value
        if k < len(starts):
            send = held["send", k]
            if FLIPPED[k]:
                gots.append(
                    lax.all_to_all(
                        send, ("rad", "lat"), 0, 0, tiled=True, axis_index_groups=flip_groups()
                    )
                )
            else:
                gots.append(lax.all_to_all(send, "lat", 0, 0, tiled=True))
        if k > 0:
            first, n = starts[k - 1]
            meta = jnp.concatenate([(lat // 8)[None], blocks, lengths[first : first + n]])
            meta = meta.astype(jnp.int32)
            by_hop = k - 1 < final
            parts = transform(gots[k - 1], legendre, meta, first, FLIPPED[k - 1], by_hop)
            if by_hop:
                moved = [
                    lax.ppermute(parts[h], "rad", rad_targets(h // Y, h % Y)) for h in range(1, 8)
                ]
                moves.append([parts[0]] + moved)
            else:
                moves.append([lax.all_to_all(parts, "rad", 0, 0, tiled=True)])
        if k > 1:
            out = put(k - 2)
    return put(final)


def solution(mesh):
    in_specs = (
        P(None, None, "rad", "lat"),
        P(),
        P("lat", None, None),
        P("lat", None, None, "rad"),
        P(),
        P("lat", "rad"),
    )
    out_specs = P("lat", None, None, "rad")
    return jax.shard_map(
        on_device, mesh=mesh, in_specs=in_specs, out_specs=out_specs, check_vma=False
    )
```

```python
import functools

import jax
import jax.numpy as jnp
from jax import lax
from jax.experimental import pallas as pl
from jax.experimental.pallas import tpu as pltpu
from jax.sharding import PartitionSpec as P

ZS, Y = 2, 4
CHUNKS = (4, 2, 2)
FLIPPED = (False, True, True)
TIES = {2: ((0, (0, 1, 2, 3, 4, 5, 7)),), 3: ((0, (6,)), (1, range(8)))}
ORDER = (6, 2, 5, 7, 1, 3, 4)
STEP = 16
BF16, F32 = jnp.bfloat16, jnp.float32


def prep_kernel(starts, per_dev, key_ref, x_ref, *refs):
    outs, (pick, swap, by_lat, by_order) = refs[: len(starts)], refs[len(starts) :]
    rows, _, orders = x_ref.shape

    @pl.when(pl.program_id(0) == 0)
    def _():
        at = 0
        for first, n in starts:
            count = 16 * n * 2
            i = lax.broadcasted_iota(jnp.int32, (count, orders), 0)
            rest, dest = i // 16, i % 16
            target = dest * (2 * per_dev) + 2 * first + rest
            hit = key_ref[...] == target
            pick[at : at + count, :] = jnp.where(hit, 1.0, 0.0).astype(BF16)
            at += count
        i = lax.broadcasted_iota(jnp.int32, (256, 256), 0)
        j = lax.broadcasted_iota(jnp.int32, (256, 256), 1)
        hit = (i // 16 == j % 16) & (i % 16 == j // 16)
        swap[...] = jnp.where(hit, 1.0, 0.0).astype(BF16)

    def to_lat(c, carry):
        at = pl.multiple_of(c * 16, 16)
        block = x_ref[pl.ds(at, 16), :, :].reshape(256, orders)
        moved = jnp.dot(swap[...], block, preferred_element_type=F32)
        by_lat[:, pl.ds(at, 16), :] = moved.astype(BF16).reshape(STEP, 16, orders)
        return carry

    lax.fori_loop(0, rows // 16, to_lat, 0, unroll=True)

    def to_order(n, carry):
        moved = lax.dot_general(
            pick[...], by_lat[n], (((1,), (1,)), ((), ())), preferred_element_type=F32
        )
        by_order[:, n] = moved.astype(BF16).reshape(by_order.shape[0], 16, rows)
        return carry

    lax.fori_loop(0, STEP, to_order, 0, unroll=True)

    base = 0
    for out, (_, n) in zip(outs, starts):
        for g in range(2 * n):
            block = by_order[base + g].reshape(256, rows)
            moved = jnp.dot(swap[...], block, preferred_element_type=F32).astype(BF16)
            out[:, g // 2, g % 2] = moved.reshape(16, STEP, rows)
        base += 2 * n


def prep(physical, pair_slot, starts, per_dev):
    orders, chans, radii, lats = physical.shape
    sent = sum(32 * n for _, n in starts)
    rows = chans * radii
    x = jnp.transpose(physical, (1, 2, 3, 0)).reshape(rows, lats, orders)
    key = (2 * pair_slot[:, None] + jnp.arange(2, dtype=jnp.int32)[None, :]).reshape(1, orders)
    return pl.pallas_call(
        functools.partial(prep_kernel, starts, per_dev),
        grid=(lats // STEP,),
        in_specs=[
            pl.BlockSpec((1, orders), lambda b: (0, 0)),
            pl.BlockSpec((rows, STEP, orders), lambda b: (0, b, 0)),
        ],
        out_specs=[
            pl.BlockSpec((16, n, 2, STEP, rows), lambda b: (0, 0, 0, b, 0)) for _, n in starts
        ],
        out_shape=[pltpu.HBM((16, n, 2, lats, rows), BF16) for _, n in starts],
        scratch_shapes=[
            pltpu.VMEM((sent, orders), BF16),
            pltpu.VMEM((256, 256), BF16),
            pltpu.VMEM((STEP, rows, orders), BF16),
            pltpu.VMEM((sent // 16, STEP, 16, rows), BF16),
        ],
        compiler_params=pltpu.CompilerParams(vmem_limit_bytes=48 << 20),
        cost_estimate=pl.CostEstimate(
            flops=2 * rows * lats * orders * (orders + 2 * sent),
            bytes_accessed=2 * rows * lats * (orders + sent),
            transcendentals=0,
        ),
        name="prep",
    )(key, x)


def spread(full, row, meta_ref, outs):
    for k in range(8):
        if len(outs) == 8:
            at = pl.multiple_of(meta_ref[1 + k] * 128, 128)
            outs[k][row] = full[:, pl.ds(at, 128)]
        else:
            outs[0][(k, *row)] = full[:, k * 128 : (k + 1) * 128]


def transform_kernel(meta_ref, got_ref, table_ref, *refs):
    outs, full = refs[:-1], refs[-1]
    slot = pl.program_id(0)
    half = table_ref.shape[2] // 2
    depth = table_ref.shape[1]
    rows = got_ref.shape[4]
    low_in = got_ref[:, 0, 0].reshape(depth, rows)
    high_in = got_ref[:, 0, 1].reshape(depth, rows)
    length = meta_ref[9 + slot]
    dims = (((0,), (0,)), ((), ()))
    low = lax.dot_general(low_in, table_ref[0], dims, preferred_element_type=F32)
    high = lax.dot_general(high_in, table_ref[0, :, half:], dims, preferred_element_type=F32)
    column = half + lax.broadcasted_iota(jnp.int32, high.shape, 1)
    full[:, :half] = low[:, :half].astype(BF16)
    full[:, half:] = jnp.where(column < length, low[:, half:], high).astype(BF16)
    spread(full, (0, 0), meta_ref, outs)


def transform_whole_kernel(meta_ref, got_ref, table_ref, *refs):
    outs, full = refs[:-1], refs[-1]
    slot, part = pl.program_id(0), pl.program_id(1)
    srcs, _, _, lats, rows = got_ref.shape
    depth, width = srcs * lats, table_ref.shape[2]
    dims = (((0,), (0,)), ((), ()))

    def product(h):
        return lax.dot_general(
            got_ref[:, 0, h].reshape(depth, rows),
            table_ref[0],
            dims,
            preferred_element_type=F32,
        )

    @pl.when(part == 0)
    def _():
        full[:, :width] = product(0).astype(BF16)

    @pl.when(part == 1)
    def _():
        column = width + lax.broadcasted_iota(jnp.int32, (rows, width), 1)
        chosen = jnp.where(column < meta_ref[9 + slot], product(0), product(1))
        full[:, width:] = chosen.astype(BF16)
        spread(full, (0,), meta_ref, outs)


def transform(got, legendre, meta, first, flipped, by_hop):
    srcs, count, _, lats, rows = got.shape
    degrees = legendre.shape[2]
    if flipped:
        kernel = transform_kernel
        depth, width = srcs // 2 * lats, degrees
        got_spec = pl.BlockSpec(
            (srcs // 2, 1, 2, lats, rows), lambda s, t, m: (t ^ m[0], s, 0, 0, 0)
        )
        table_spec = pl.BlockSpec((1, depth, width), lambda s, t, m: (first + s, t ^ m[0], 0))
        shape, block = (2, count, rows, 128), (1, 1, rows, 128)
        where = lambda s, t, m: (t, s, 0, 0)
    else:
        kernel = transform_whole_kernel
        depth, width = srcs * lats, degrees // 2
        got_spec = pl.BlockSpec((srcs, 1, 2, lats, rows), lambda s, t, m: (0, s, 0, 0, 0))
        table_spec = pl.BlockSpec((1, depth, width), lambda s, t, m: (first + s, 0, t))
        shape, block = (count, rows, 128), (1, rows, 128)
        where = lambda s, t, m: (s, 0, 0)
    if by_hop:
        out_specs = [pl.BlockSpec(block, where)] * 8
        out_shape = [pltpu.HBM(shape, BF16)] * 8
    else:
        out_specs = pl.BlockSpec((8,) + block, lambda s, t, m: (0, *where(s, t, m)))
        out_shape = pltpu.HBM((8,) + shape, BF16)
    return pl.pallas_call(
        kernel,
        grid_spec=pltpu.PrefetchScalarGridSpec(
            num_scalar_prefetch=1,
            grid=(count, 2),
            in_specs=[got_spec, table_spec],
            out_specs=out_specs,
            scratch_shapes=[pltpu.VMEM((rows, degrees), BF16)],
        ),
        out_shape=out_shape,
        compiler_params=pltpu.CompilerParams(vmem_limit_bytes=48 << 20),
        cost_estimate=pl.CostEstimate(
            flops=3 * count * rows * srcs * lats * degrees,
            bytes_accessed=2 * count * srcs * lats * (2 * rows + degrees),
            transcendentals=0,
        ),
        name="transform",
    )(meta, pltpu.with_memory_space_constraint(got, pltpu.HBM), legendre)


def invert(row, inv_ref, out_ref, side):
    row = jnp.concatenate([row, row], axis=1)
    for q in range(4):
        every = inv_ref[q].reshape(4 * 256, 256)
        found = jnp.dot(every, side[q], preferred_element_type=F32)
        acc = found[:256]
        for g in range(1, 4):
            acc = jnp.where(row == g, found[g * 256 : (g + 1) * 256], acc)
        acc = acc.astype(BF16)
        out_ref[0, 2 * q] = acc[:, :128]
        out_ref[0, 2 * q + 1] = acc[:, 128:]


def settle_kernel(first, flipped, meta_ref, *refs):
    parts = refs[:-5]
    state_ref, index_ref, inv_ref, out_ref, side = refs[-5:]
    radii = 32

    def part(zs, ys, *where):
        if len(parts) == 8:
            return parts[zs * Y + ys][where].astype(F32)
        return parts[0][(zs * Y + ys, *where)].astype(F32)

    for zs in range(ZS):
        for ys in range(Y):
            at = (zs * Y + ys) * radii
            if len(parts) == 8:
                zl, y = meta_ref[0], meta_ref[1]
                at = pl.multiple_of(((zl ^ zs) * Y + lax.rem(y + (Y - ys), Y)) * radii, radii)
            for c in range(8):
                rows = slice(c * radii, (c + 1) * radii)
                if flipped:
                    total = part(zs, ys, 0, 0, rows) + part(1 - zs, ys, 1, 0, rows)
                else:
                    total = part(zs, ys, 0, rows)
                value = state_ref[0, c, pl.ds(at, radii), :].astype(F32) + 0.5 * total
                lanes = slice((c % 2) * 128, (c % 2) * 128 + 128)
                side[c // 2, pl.ds(at, radii), lanes] = value.astype(BF16)
    invert(index_ref[pl.ds(first + pl.program_id(0), 1), :], inv_ref, out_ref, side)


def settle_chained_kernel(first, flipped, meta_ref, *refs):
    settle_kernel(first, flipped, meta_ref, *refs[:-3], *refs[-2:])


def settle(parts, state, inverses, index, meta, first, count, flipped, so_far):
    shape = parts[0].shape
    block = [1 if i == len(shape) - 3 else n for i, n in enumerate(shape)]
    lead = (0,) * (len(shape) - 3)
    operands = [meta, *parts, state, index, inverses]
    in_specs = [pl.BlockSpec(block, lambda s, m: (*lead, s, 0, 0))] * len(parts) + [
        pl.BlockSpec((1,) + state.shape[1:], lambda s, m: (first + s, 0, 0, 0)),
        pl.BlockSpec(index.shape, lambda s, m: (0, 0)),
        pl.BlockSpec(inverses.shape, lambda s, m: (0, 0, 0, 0)),
    ]
    kernel = settle_kernel if so_far is None else settle_chained_kernel
    aliases = {}
    if so_far is not None:
        operands.append(so_far)
        in_specs.append(pl.BlockSpec(memory_space=pl.ANY))
        aliases = {len(operands) - 1: 0}
    return pl.pallas_call(
        functools.partial(kernel, first, flipped),
        grid_spec=pltpu.PrefetchScalarGridSpec(
            num_scalar_prefetch=1,
            grid=(count,),
            in_specs=in_specs,
            out_specs=pl.BlockSpec((1,) + state.shape[1:], lambda s, m: (first + s, 0, 0, 0)),
            scratch_shapes=[pltpu.VMEM((4, 256, 256), BF16)],
        ),
        out_shape=jax.ShapeDtypeStruct(state.shape, BF16),
        input_output_aliases=aliases,
        compiler_params=pltpu.CompilerParams(vmem_limit_bytes=48 << 20),
        cost_estimate=pl.CostEstimate(
            flops=2 * count * 16 * 256 * 256 * 256,
            bytes_accessed=count * (2 << 20) + (2 << 20),
            transcendentals=0,
        ),
        name="settle",
    )(*operands)


def flip_groups():
    groups = []
    for y in range(Y):
        for zl in range(ZS):
            groups.append([((zl ^ (l // 8)) * Y + y) * 16 + l for l in range(16)])
    return groups


def rad_targets(kz, ky):
    return [(i, ((i // Y) ^ kz) * Y + (i % Y + ky) % Y) for i in range(ZS * Y)]


def on_device(physical, pair_slot, legendre, spectral_state, inverses, block_index):
    pair_count = pair_slot.shape[0]
    per_dev, _, degrees = legendre.shape
    starts, first = [], 0
    for n in CHUNKS:
        starts.append((first, n))
        first += n
    sends = list(prep(physical, pair_slot, tuple(starts), per_dev))

    lat, rad = lax.axis_index("lat"), lax.axis_index("rad")
    zl, y = rad // Y, rad % Y
    slots = lat * per_dev + jnp.arange(per_dev, dtype=jnp.int32)
    matches = pair_slot[None, :] == slots[:, None]
    owners = jnp.sum(jnp.where(matches, jnp.arange(pair_count, dtype=jnp.int32), 0), axis=1)
    stride = degrees // 2 // pair_count
    lengths = degrees - (1 + owners * stride)
    hops = jnp.arange(8, dtype=jnp.int32)
    blocks = (zl ^ (hops // Y)) * Y + (y + hops) % Y
    place = jnp.stack([zl, y]).astype(jnp.int32)

    out, gots, moves = None, [], []

    final = len(starts) - 1

    def put(k):
        return settle(
            moves[k],
            spectral_state,
            inverses,
            block_index,
            place,
            *starts[k],
            FLIPPED[k],
            out,
        )

    for k in range(len(starts) + 1):
        keep = {}
        if k > 0:
            keep["got", k - 1] = gots[k - 1]
        for chunk, hops_of in TIES.get(k, ()):
            for h in hops_of:
                keep["move", chunk, h] = moves[chunk][h]
        if k > 2:
            keep["out"] = out
        if k < len(starts):
            keep["send", k] = sends[k]
        held = dict(zip(keep, lax.optimization_barrier(tuple(keep.values()))))
        out = held.get("out", out)
        if k > 0:
            gots[k - 1] = held["got", k - 1]
        for name, value in held.items():
            if name[0] == "move":
                moves[name[1]][name[2]] = value
        if k < len(starts):
            send = held["send", k]
            if FLIPPED[k]:
                gots.append(
                    lax.all_to_all(
                        send, ("rad", "lat"), 0, 0, tiled=True, axis_index_groups=flip_groups()
                    )
                )
            else:
                gots.append(lax.all_to_all(send, "lat", 0, 0, tiled=True))
        if k > 0:
            first, n = starts[k - 1]
            meta = jnp.concatenate([(lat // 8)[None], blocks, lengths[first : first + n]])
            meta = meta.astype(jnp.int32)
            by_hop = True
            parts = transform(gots[k - 1], legendre, meta, first, FLIPPED[k - 1], by_hop)
            if by_hop:
                moved = {0: parts[0]}
                for h in ORDER:
                    moved[h] = lax.ppermute(parts[h], "rad", rad_targets(h // Y, h % Y))
                moves.append([moved[h] for h in range(8)])
            else:
                moves.append([lax.all_to_all(parts, "rad", 0, 0, tiled=True)])
        if k > 1:
            out = put(k - 2)
    return put(final)


def solution(mesh):
    in_specs = (
        P(None, None, "rad", "lat"),
        P(),
        P("lat", None, None),
        P("lat", None, None, "rad"),
        P(),
        P("lat", "rad"),
    )
    out_specs = P("lat", None, None, "rad")
    return jax.shard_map(
        on_device, mesh=mesh, in_specs=in_specs, out_specs=out_specs, check_vma=False
    )
```

```python
import functools

import jax
import jax.numpy as jnp
from jax import lax
from jax.experimental import pallas as pl
from jax.experimental.pallas import tpu as pltpu
from jax.sharding import PartitionSpec as P

ZS, Y = 2, 4
CHUNKS = (4, 2, 2)
FLIPPED = (False, True, True)
TIES = {2: ((0, (0, 1, 2, 3, 4, 5, 7)),), 3: ((0, (6,)), (1, range(8)), (2, range(8)))}
UNITS = ((0, 0, 4), (1, 0, 1), (1, 1, 1), (2, 0, 1), (2, 1, 1))
ORDER = (6, 2, 5, 7, 1, 3, 4)
STEP = 16
BF16, F32 = jnp.bfloat16, jnp.float32


def prep_kernel(starts, per_dev, key_ref, x_ref, *refs):
    outs, (pick, swap, by_lat, by_order) = refs[: len(starts)], refs[len(starts) :]
    rows, _, orders = x_ref.shape

    @pl.when(pl.program_id(0) == 0)
    def _():
        at = 0
        for first, n in starts:
            count = 16 * n * 2
            i = lax.broadcasted_iota(jnp.int32, (count, orders), 0)
            rest, dest = i // 16, i % 16
            target = dest * (2 * per_dev) + 2 * first + rest
            hit = key_ref[...] == target
            pick[at : at + count, :] = jnp.where(hit, 1.0, 0.0).astype(BF16)
            at += count
        i = lax.broadcasted_iota(jnp.int32, (256, 256), 0)
        j = lax.broadcasted_iota(jnp.int32, (256, 256), 1)
        hit = (i // 16 == j % 16) & (i % 16 == j // 16)
        swap[...] = jnp.where(hit, 1.0, 0.0).astype(BF16)

    def to_lat(c, carry):
        at = pl.multiple_of(c * 16, 16)
        block = x_ref[pl.ds(at, 16), :, :].reshape(256, orders)
        moved = jnp.dot(swap[...], block, preferred_element_type=F32)
        by_lat[:, pl.ds(at, 16), :] = moved.astype(BF16).reshape(STEP, 16, orders)
        return carry

    lax.fori_loop(0, rows // 16, to_lat, 0, unroll=True)

    def to_order(n, carry):
        moved = lax.dot_general(
            pick[...], by_lat[n], (((1,), (1,)), ((), ())), preferred_element_type=F32
        )
        by_order[:, n] = moved.astype(BF16).reshape(by_order.shape[0], 16, rows)
        return carry

    lax.fori_loop(0, STEP, to_order, 0, unroll=True)

    base = 0
    for out, (_, n) in zip(outs, starts):
        for g in range(2 * n):
            block = by_order[base + g].reshape(256, rows)
            moved = jnp.dot(swap[...], block, preferred_element_type=F32).astype(BF16)
            out[:, g // 2, g % 2] = moved.reshape(16, STEP, rows)
        base += 2 * n


def prep(physical, pair_slot, starts, per_dev):
    orders, chans, radii, lats = physical.shape
    sent = sum(32 * n for _, n in starts)
    rows = chans * radii
    x = jnp.transpose(physical, (1, 2, 3, 0)).reshape(rows, lats, orders)
    key = (2 * pair_slot[:, None] + jnp.arange(2, dtype=jnp.int32)[None, :]).reshape(1, orders)
    return pl.pallas_call(
        functools.partial(prep_kernel, starts, per_dev),
        grid=(lats // STEP,),
        in_specs=[
            pl.BlockSpec((1, orders), lambda b: (0, 0)),
            pl.BlockSpec((rows, STEP, orders), lambda b: (0, b, 0)),
        ],
        out_specs=[
            pl.BlockSpec((16, n, 2, STEP, rows), lambda b: (0, 0, 0, b, 0)) for _, n in starts
        ],
        out_shape=[pltpu.HBM((16, n, 2, lats, rows), BF16) for _, n in starts],
        scratch_shapes=[
            pltpu.VMEM((sent, orders), BF16),
            pltpu.VMEM((256, 256), BF16),
            pltpu.VMEM((STEP, rows, orders), BF16),
            pltpu.VMEM((sent // 16, STEP, 16, rows), BF16),
        ],
        compiler_params=pltpu.CompilerParams(vmem_limit_bytes=48 << 20),
        cost_estimate=pl.CostEstimate(
            flops=2 * rows * lats * orders * (orders + 2 * sent),
            bytes_accessed=2 * rows * lats * (orders + sent),
            transcendentals=0,
        ),
        name="prep",
    )(key, x)


def spread(full, row, meta_ref, outs):
    for k in range(8):
        if len(outs) == 8:
            at = pl.multiple_of(meta_ref[1 + k] * 128, 128)
            outs[k][row] = full[:, pl.ds(at, 128)]
        else:
            outs[0][(k, *row)] = full[:, k * 128 : (k + 1) * 128]


def transform_kernel(meta_ref, got_ref, table_ref, *refs):
    outs, full = refs[:-1], refs[-1]
    slot = pl.program_id(0)
    half = table_ref.shape[2] // 2
    depth = table_ref.shape[1]
    rows = got_ref.shape[4]
    low_in = got_ref[:, 0, 0].reshape(depth, rows)
    high_in = got_ref[:, 0, 1].reshape(depth, rows)
    length = meta_ref[9 + slot]
    dims = (((0,), (0,)), ((), ()))
    low = lax.dot_general(low_in, table_ref[0], dims, preferred_element_type=F32)
    high = lax.dot_general(high_in, table_ref[0, :, half:], dims, preferred_element_type=F32)
    column = half + lax.broadcasted_iota(jnp.int32, high.shape, 1)
    full[:, :half] = low[:, :half].astype(BF16)
    full[:, half:] = jnp.where(column < length, low[:, half:], high).astype(BF16)
    spread(full, (0, 0), meta_ref, outs)


def transform_whole_kernel(meta_ref, got_ref, table_ref, *refs):
    outs, full = refs[:-1], refs[-1]
    slot, part = pl.program_id(0), pl.program_id(1)
    srcs, _, _, lats, rows = got_ref.shape
    depth, width = srcs * lats, table_ref.shape[2]
    dims = (((0,), (0,)), ((), ()))

    def product(h):
        return lax.dot_general(
            got_ref[:, 0, h].reshape(depth, rows),
            table_ref[0],
            dims,
            preferred_element_type=F32,
        )

    @pl.when(part == 0)
    def _():
        full[:, :width] = product(0).astype(BF16)

    @pl.when(part == 1)
    def _():
        column = width + lax.broadcasted_iota(jnp.int32, (rows, width), 1)
        chosen = jnp.where(column < meta_ref[9 + slot], product(0), product(1))
        full[:, width:] = chosen.astype(BF16)
        spread(full, (0,), meta_ref, outs)


def transform(got, legendre, meta, first, offset, count, flipped):
    srcs, _, _, lats, rows = got.shape
    degrees = legendre.shape[2]
    if flipped:
        kernel = transform_kernel
        depth, width = srcs // 2 * lats, degrees
        got_spec = pl.BlockSpec(
            (srcs // 2, 1, 2, lats, rows), lambda s, t, m: (t ^ m[0], offset + s, 0, 0, 0)
        )
        table_spec = pl.BlockSpec((1, depth, width), lambda s, t, m: (first + s, t ^ m[0], 0))
        shape, block = (2, count, rows, 128), (1, 1, rows, 128)
        where = lambda s, t, m: (t, s, 0, 0)
    else:
        kernel = transform_whole_kernel
        depth, width = srcs * lats, degrees // 2
        got_spec = pl.BlockSpec((srcs, 1, 2, lats, rows), lambda s, t, m: (0, offset + s, 0, 0, 0))
        table_spec = pl.BlockSpec((1, depth, width), lambda s, t, m: (first + s, 0, t))
        shape, block = (count, rows, 128), (1, rows, 128)
        where = lambda s, t, m: (s, 0, 0)
    out_specs = [pl.BlockSpec(block, where)] * 8
    out_shape = [pltpu.HBM(shape, BF16)] * 8
    return pl.pallas_call(
        kernel,
        grid_spec=pltpu.PrefetchScalarGridSpec(
            num_scalar_prefetch=1,
            grid=(count, 2),
            in_specs=[got_spec, table_spec],
            out_specs=out_specs,
            scratch_shapes=[pltpu.VMEM((rows, degrees), BF16)],
        ),
        out_shape=out_shape,
        compiler_params=pltpu.CompilerParams(vmem_limit_bytes=48 << 20),
        cost_estimate=pl.CostEstimate(
            flops=3 * count * rows * srcs * lats * degrees,
            bytes_accessed=2 * count * srcs * lats * (2 * rows + degrees),
            transcendentals=0,
        ),
        name="transform",
    )(meta, pltpu.with_memory_space_constraint(got, pltpu.HBM), legendre)


def invert(row, inv_ref, out_ref, side):
    row = jnp.concatenate([row, row], axis=1)
    for q in range(4):
        every = inv_ref[q].reshape(4 * 256, 256)
        found = jnp.dot(every, side[q], preferred_element_type=F32)
        acc = found[:256]
        for g in range(1, 4):
            acc = jnp.where(row == g, found[g * 256 : (g + 1) * 256], acc)
        acc = acc.astype(BF16)
        out_ref[0, 2 * q] = acc[:, :128]
        out_ref[0, 2 * q + 1] = acc[:, 128:]


def settle_kernel(first, flipped, meta_ref, *refs):
    parts = refs[:-5]
    state_ref, index_ref, inv_ref, out_ref, side = refs[-5:]
    radii = 32

    def part(zs, ys, *where):
        if len(parts) == 8:
            return parts[zs * Y + ys][where].astype(F32)
        return parts[0][(zs * Y + ys, *where)].astype(F32)

    for zs in range(ZS):
        for ys in range(Y):
            at = (zs * Y + ys) * radii
            if len(parts) == 8:
                zl, y = meta_ref[0], meta_ref[1]
                at = pl.multiple_of(((zl ^ zs) * Y + lax.rem(y + (Y - ys), Y)) * radii, radii)
            for c in range(8):
                rows = slice(c * radii, (c + 1) * radii)
                if flipped:
                    total = part(zs, ys, 0, 0, rows) + part(1 - zs, ys, 1, 0, rows)
                else:
                    total = part(zs, ys, 0, rows)
                value = state_ref[0, c, pl.ds(at, radii), :].astype(F32) + 0.5 * total
                lanes = slice((c % 2) * 128, (c % 2) * 128 + 128)
                side[c // 2, pl.ds(at, radii), lanes] = value.astype(BF16)
    invert(index_ref[pl.ds(first + pl.program_id(0), 1), :], inv_ref, out_ref, side)


def settle_chained_kernel(first, flipped, meta_ref, *refs):
    settle_kernel(first, flipped, meta_ref, *refs[:-3], *refs[-2:])


def settle(parts, state, inverses, index, meta, first, count, flipped, so_far):
    shape = parts[0].shape
    block = [1 if i == len(shape) - 3 else n for i, n in enumerate(shape)]
    lead = (0,) * (len(shape) - 3)
    operands = [meta, *parts, state, index, inverses]
    in_specs = [pl.BlockSpec(block, lambda s, m: (*lead, s, 0, 0))] * len(parts) + [
        pl.BlockSpec((1,) + state.shape[1:], lambda s, m: (first + s, 0, 0, 0)),
        pl.BlockSpec(index.shape, lambda s, m: (0, 0)),
        pl.BlockSpec(inverses.shape, lambda s, m: (0, 0, 0, 0)),
    ]
    kernel = settle_kernel if so_far is None else settle_chained_kernel
    aliases = {}
    if so_far is not None:
        operands.append(so_far)
        in_specs.append(pl.BlockSpec(memory_space=pl.ANY))
        aliases = {len(operands) - 1: 0}
    return pl.pallas_call(
        functools.partial(kernel, first, flipped),
        grid_spec=pltpu.PrefetchScalarGridSpec(
            num_scalar_prefetch=1,
            grid=(count,),
            in_specs=in_specs,
            out_specs=pl.BlockSpec((1,) + state.shape[1:], lambda s, m: (first + s, 0, 0, 0)),
            scratch_shapes=[pltpu.VMEM((4, 256, 256), BF16)],
        ),
        out_shape=jax.ShapeDtypeStruct(state.shape, BF16),
        input_output_aliases=aliases,
        compiler_params=pltpu.CompilerParams(vmem_limit_bytes=48 << 20),
        cost_estimate=pl.CostEstimate(
            flops=2 * count * 16 * 256 * 256 * 256,
            bytes_accessed=count * (2 << 20) + (2 << 20),
            transcendentals=0,
        ),
        name="settle",
    )(*operands)


def flip_groups():
    groups = []
    for y in range(Y):
        for zl in range(ZS):
            groups.append([((zl ^ (l // 8)) * Y + y) * 16 + l for l in range(16)])
    return groups


def rad_targets(kz, ky):
    return [(i, ((i // Y) ^ kz) * Y + (i % Y + ky) % Y) for i in range(ZS * Y)]


def on_device(physical, pair_slot, legendre, spectral_state, inverses, block_index):
    pair_count = pair_slot.shape[0]
    per_dev, _, degrees = legendre.shape
    starts, first = [], 0
    for n in CHUNKS:
        starts.append((first, n))
        first += n
    sends = list(prep(physical, pair_slot, tuple(starts), per_dev))

    lat, rad = lax.axis_index("lat"), lax.axis_index("rad")
    zl, y = rad // Y, rad % Y
    slots = lat * per_dev + jnp.arange(per_dev, dtype=jnp.int32)
    matches = pair_slot[None, :] == slots[:, None]
    owners = jnp.sum(jnp.where(matches, jnp.arange(pair_count, dtype=jnp.int32), 0), axis=1)
    stride = degrees // 2 // pair_count
    lengths = degrees - (1 + owners * stride)
    hops = jnp.arange(8, dtype=jnp.int32)
    blocks = (zl ^ (hops // Y)) * Y + (y + hops) % Y
    place = jnp.stack([zl, y]).astype(jnp.int32)

    out, gots, moves = None, [], []

    def put(u):
        chunk, offset, count = UNITS[u]
        return settle(
            moves[u],
            spectral_state,
            inverses,
            block_index,
            place,
            starts[chunk][0] + offset,
            count,
            FLIPPED[chunk],
            out,
        )

    for k in range(len(starts) + 1):
        keep = {}
        if k > 0:
            keep["got", k - 1] = gots[k - 1]
        for unit, hops_of in TIES.get(k, ()):
            for h in hops_of:
                keep["move", unit, h] = moves[unit][h]
        if k > 2:
            keep["out"] = out
        if k < len(starts):
            keep["send", k] = sends[k]
        held = dict(zip(keep, lax.optimization_barrier(tuple(keep.values()))))
        out = held.get("out", out)
        if k > 0:
            gots[k - 1] = held["got", k - 1]
        for name, value in held.items():
            if name[0] == "move":
                moves[name[1]][name[2]] = value
        if k < len(starts):
            send = held["send", k]
            if FLIPPED[k]:
                gots.append(
                    lax.all_to_all(
                        send, ("rad", "lat"), 0, 0, tiled=True, axis_index_groups=flip_groups()
                    )
                )
            else:
                gots.append(lax.all_to_all(send, "lat", 0, 0, tiled=True))
        for chunk, offset, count in UNITS:
            if chunk == k - 1:
                first = starts[chunk][0] + offset
                meta = jnp.concatenate([(lat // 8)[None], blocks, lengths[first : first + count]])
                parts = transform(
                    gots[chunk],
                    legendre,
                    meta.astype(jnp.int32),
                    first,
                    offset,
                    count,
                    FLIPPED[chunk],
                )
                moved = {0: parts[0]}
                for h in ORDER:
                    moved[h] = lax.ppermute(parts[h], "rad", rad_targets(h // Y, h % Y))
                moves.append([moved[h] for h in range(8)])
        for u, (chunk, _, _) in enumerate(UNITS):
            if chunk == k - 2:
                out = put(u)
    for u, (chunk, _, _) in enumerate(UNITS):
        if chunk == len(starts) - 1:
            out = put(u)
    return out


def solution(mesh):
    in_specs = (
        P(None, None, "rad", "lat"),
        P(),
        P("lat", None, None),
        P("lat", None, None, "rad"),
        P(),
        P("lat", "rad"),
    )
    out_specs = P("lat", None, None, "rad")
    return jax.shard_map(
        on_device, mesh=mesh, in_specs=in_specs, out_specs=out_specs, check_vma=False
    )
```

```python
import functools

import jax
import jax.numpy as jnp
from jax import lax
from jax.experimental import pallas as pl
from jax.experimental.pallas import tpu as pltpu
from jax.sharding import PartitionSpec as P

ZS, Y = 2, 4
CHUNKS = (4, 2, 2)
FLIPPED = (False, True, False)
TIES = {2: ((0, (0, 1, 2, 3, 4, 5, 7)),), 3: ((0, (6,)), (1, (0, 1, 2, 3)))}
ORDER = (6, 2, 5, 7, 1, 3, 4)
STEP = 16
BF16, F32 = jnp.bfloat16, jnp.float32


def prep_kernel(starts, per_dev, key_ref, x_ref, *refs):
    outs, (pick, swap, by_lat, by_order) = refs[: len(starts)], refs[len(starts) :]
    rows, _, orders = x_ref.shape

    @pl.when(pl.program_id(0) == 0)
    def _():
        at = 0
        for first, n in starts:
            count = 16 * n * 2
            i = lax.broadcasted_iota(jnp.int32, (count, orders), 0)
            rest, dest = i // 16, i % 16
            target = dest * (2 * per_dev) + 2 * first + rest
            hit = key_ref[...] == target
            pick[at : at + count, :] = jnp.where(hit, 1.0, 0.0).astype(BF16)
            at += count
        i = lax.broadcasted_iota(jnp.int32, (256, 256), 0)
        j = lax.broadcasted_iota(jnp.int32, (256, 256), 1)
        hit = (i // 16 == j % 16) & (i % 16 == j // 16)
        swap[...] = jnp.where(hit, 1.0, 0.0).astype(BF16)

    def to_lat(c, carry):
        at = pl.multiple_of(c * 16, 16)
        block = x_ref[pl.ds(at, 16), :, :].reshape(256, orders)
        moved = jnp.dot(swap[...], block, preferred_element_type=F32)
        by_lat[:, pl.ds(at, 16), :] = moved.astype(BF16).reshape(STEP, 16, orders)
        return carry

    lax.fori_loop(0, rows // 16, to_lat, 0, unroll=True)

    def to_order(n, carry):
        moved = lax.dot_general(
            pick[...], by_lat[n], (((1,), (1,)), ((), ())), preferred_element_type=F32
        )
        by_order[:, n] = moved.astype(BF16).reshape(by_order.shape[0], 16, rows)
        return carry

    lax.fori_loop(0, STEP, to_order, 0, unroll=True)

    base = 0
    for out, (_, n) in zip(outs, starts):
        for g in range(2 * n):
            block = by_order[base + g].reshape(256, rows)
            moved = jnp.dot(swap[...], block, preferred_element_type=F32).astype(BF16)
            out[:, g // 2, g % 2] = moved.reshape(16, STEP, rows)
        base += 2 * n


def prep(physical, pair_slot, starts, per_dev):
    orders, chans, radii, lats = physical.shape
    sent = sum(32 * n for _, n in starts)
    rows = chans * radii
    x = jnp.transpose(physical, (1, 2, 3, 0)).reshape(rows, lats, orders)
    key = (2 * pair_slot[:, None] + jnp.arange(2, dtype=jnp.int32)[None, :]).reshape(1, orders)
    return pl.pallas_call(
        functools.partial(prep_kernel, starts, per_dev),
        grid=(lats // STEP,),
        in_specs=[
            pl.BlockSpec((1, orders), lambda b: (0, 0)),
            pl.BlockSpec((rows, STEP, orders), lambda b: (0, b, 0)),
        ],
        out_specs=[
            pl.BlockSpec((16, n, 2, STEP, rows), lambda b: (0, 0, 0, b, 0)) for _, n in starts
        ],
        out_shape=[pltpu.HBM((16, n, 2, lats, rows), BF16) for _, n in starts],
        scratch_shapes=[
            pltpu.VMEM((sent, orders), BF16),
            pltpu.VMEM((256, 256), BF16),
            pltpu.VMEM((STEP, rows, orders), BF16),
            pltpu.VMEM((sent // 16, STEP, 16, rows), BF16),
        ],
        compiler_params=pltpu.CompilerParams(vmem_limit_bytes=48 << 20),
        cost_estimate=pl.CostEstimate(
            flops=2 * rows * lats * orders * (orders + 2 * sent),
            bytes_accessed=2 * rows * lats * (orders + sent),
            transcendentals=0,
        ),
        name="prep",
    )(key, x)


def spread(full, row, meta_ref, outs):
    for k in range(8):
        if len(outs) == 8:
            at = pl.multiple_of(meta_ref[1 + k] * 128, 128)
            outs[k][row] = full[:, pl.ds(at, 128)]
        else:
            outs[0][(k, *row)] = full[:, k * 128 : (k + 1) * 128]


def transform_kernel(meta_ref, got_ref, table_ref, *refs):
    outs, full = refs[:-1], refs[-1]
    slot = pl.program_id(0)
    half = table_ref.shape[2] // 2
    depth = table_ref.shape[1]
    rows = got_ref.shape[4]
    low_in = got_ref[:, 0, 0].reshape(depth, rows)
    high_in = got_ref[:, 0, 1].reshape(depth, rows)
    length = meta_ref[9 + slot]
    dims = (((0,), (0,)), ((), ()))
    low = lax.dot_general(low_in, table_ref[0], dims, preferred_element_type=F32)
    high = lax.dot_general(high_in, table_ref[0, :, half:], dims, preferred_element_type=F32)
    column = half + lax.broadcasted_iota(jnp.int32, high.shape, 1)
    full[:, :half] = low[:, :half].astype(BF16)
    full[:, half:] = jnp.where(column < length, low[:, half:], high).astype(BF16)
    spread(full, (0, 0), meta_ref, outs)


def transform_whole_kernel(meta_ref, got_ref, table_ref, *refs):
    outs, full = refs[:-1], refs[-1]
    slot, part = pl.program_id(0), pl.program_id(1)
    srcs, _, _, lats, rows = got_ref.shape
    depth, width = srcs * lats, table_ref.shape[2]
    dims = (((0,), (0,)), ((), ()))

    def product(h):
        return lax.dot_general(
            got_ref[:, 0, h].reshape(depth, rows),
            table_ref[0],
            dims,
            preferred_element_type=F32,
        )

    @pl.when(part == 0)
    def _():
        full[:, :width] = product(0).astype(BF16)

    @pl.when(part == 1)
    def _():
        column = width + lax.broadcasted_iota(jnp.int32, (rows, width), 1)
        chosen = jnp.where(column < meta_ref[9 + slot], product(0), product(1))
        full[:, width:] = chosen.astype(BF16)
        spread(full, (0,), meta_ref, outs)


def transform(got, legendre, meta, first, flipped, by_hop):
    srcs, count, _, lats, rows = got.shape
    degrees = legendre.shape[2]
    if flipped:
        kernel = transform_kernel
        depth, width = srcs // 2 * lats, degrees
        got_spec = pl.BlockSpec(
            (srcs // 2, 1, 2, lats, rows), lambda s, t, m: (t ^ m[0], s, 0, 0, 0)
        )
        table_spec = pl.BlockSpec((1, depth, width), lambda s, t, m: (first + s, t ^ m[0], 0))
        shape, block = (2, count, rows, 128), (1, 1, rows, 128)
        where = lambda s, t, m: (t, s, 0, 0)
    else:
        kernel = transform_whole_kernel
        depth, width = srcs * lats, degrees // 2
        got_spec = pl.BlockSpec((srcs, 1, 2, lats, rows), lambda s, t, m: (0, s, 0, 0, 0))
        table_spec = pl.BlockSpec((1, depth, width), lambda s, t, m: (first + s, 0, t))
        shape, block = (count, rows, 128), (1, rows, 128)
        where = lambda s, t, m: (s, 0, 0)
    if by_hop:
        out_specs = [pl.BlockSpec(block, where)] * 8
        out_shape = [pltpu.HBM(shape, BF16)] * 8
    else:
        out_specs = pl.BlockSpec((8,) + block, lambda s, t, m: (0, *where(s, t, m)))
        out_shape = pltpu.HBM((8,) + shape, BF16)
    return pl.pallas_call(
        kernel,
        grid_spec=pltpu.PrefetchScalarGridSpec(
            num_scalar_prefetch=1,
            grid=(count, 2),
            in_specs=[got_spec, table_spec],
            out_specs=out_specs,
            scratch_shapes=[pltpu.VMEM((rows, degrees), BF16)],
        ),
        out_shape=out_shape,
        compiler_params=pltpu.CompilerParams(vmem_limit_bytes=48 << 20),
        cost_estimate=pl.CostEstimate(
            flops=3 * count * rows * srcs * lats * degrees,
            bytes_accessed=2 * count * srcs * lats * (2 * rows + degrees),
            transcendentals=0,
        ),
        name="transform",
    )(meta, pltpu.with_memory_space_constraint(got, pltpu.HBM), legendre)


def invert(row, inv_ref, out_ref, side):
    row = jnp.concatenate([row, row], axis=1)
    for q in range(4):
        every = inv_ref[q].reshape(4 * 256, 256)
        found = jnp.dot(every, side[q], preferred_element_type=F32)
        acc = found[:256]
        for g in range(1, 4):
            acc = jnp.where(row == g, found[g * 256 : (g + 1) * 256], acc)
        acc = acc.astype(BF16)
        out_ref[0, 2 * q] = acc[:, :128]
        out_ref[0, 2 * q + 1] = acc[:, 128:]


def settle_kernel(first, flipped, meta_ref, *refs):
    parts = refs[:-5]
    state_ref, index_ref, inv_ref, out_ref, side = refs[-5:]
    radii = 32

    def part(zs, ys, *where):
        if len(parts) == 8:
            return parts[zs * Y + ys][where].astype(F32)
        return parts[0][(zs * Y + ys, *where)].astype(F32)

    for zs in range(ZS):
        for ys in range(Y):
            at = (zs * Y + ys) * radii
            if len(parts) == 8:
                zl, y = meta_ref[0], meta_ref[1]
                at = pl.multiple_of(((zl ^ zs) * Y + lax.rem(y + (Y - ys), Y)) * radii, radii)
            for c in range(8):
                rows = slice(c * radii, (c + 1) * radii)
                if flipped:
                    total = part(zs, ys, 0, 0, rows) + part(1 - zs, ys, 1, 0, rows)
                else:
                    total = part(zs, ys, 0, rows)
                value = state_ref[0, c, pl.ds(at, radii), :].astype(F32) + 0.5 * total
                lanes = slice((c % 2) * 128, (c % 2) * 128 + 128)
                side[c // 2, pl.ds(at, radii), lanes] = value.astype(BF16)
    invert(index_ref[pl.ds(first + pl.program_id(0), 1), :], inv_ref, out_ref, side)


def settle_chained_kernel(first, flipped, meta_ref, *refs):
    settle_kernel(first, flipped, meta_ref, *refs[:-3], *refs[-2:])


def settle(parts, state, inverses, index, meta, first, count, flipped, so_far):
    shape = parts[0].shape
    block = [1 if i == len(shape) - 3 else n for i, n in enumerate(shape)]
    lead = (0,) * (len(shape) - 3)
    operands = [meta, *parts, state, index, inverses]
    in_specs = [pl.BlockSpec(block, lambda s, m: (*lead, s, 0, 0))] * len(parts) + [
        pl.BlockSpec((1,) + state.shape[1:], lambda s, m: (first + s, 0, 0, 0)),
        pl.BlockSpec(index.shape, lambda s, m: (0, 0)),
        pl.BlockSpec(inverses.shape, lambda s, m: (0, 0, 0, 0)),
    ]
    kernel = settle_kernel if so_far is None else settle_chained_kernel
    aliases = {}
    if so_far is not None:
        operands.append(so_far)
        in_specs.append(pl.BlockSpec(memory_space=pl.ANY))
        aliases = {len(operands) - 1: 0}
    return pl.pallas_call(
        functools.partial(kernel, first, flipped),
        grid_spec=pltpu.PrefetchScalarGridSpec(
            num_scalar_prefetch=1,
            grid=(count,),
            in_specs=in_specs,
            out_specs=pl.BlockSpec((1,) + state.shape[1:], lambda s, m: (first + s, 0, 0, 0)),
            scratch_shapes=[pltpu.VMEM((4, 256, 256), BF16)],
        ),
        out_shape=jax.ShapeDtypeStruct(state.shape, BF16),
        input_output_aliases=aliases,
        compiler_params=pltpu.CompilerParams(vmem_limit_bytes=48 << 20),
        cost_estimate=pl.CostEstimate(
            flops=2 * count * 16 * 256 * 256 * 256,
            bytes_accessed=count * (2 << 20) + (2 << 20),
            transcendentals=0,
        ),
        name="settle",
    )(*operands)


def flip_groups():
    groups = []
    for y in range(Y):
        for zl in range(ZS):
            groups.append([((zl ^ (l // 8)) * Y + y) * 16 + l for l in range(16)])
    return groups


def rad_targets(kz, ky):
    return [(i, ((i // Y) ^ kz) * Y + (i % Y + ky) % Y) for i in range(ZS * Y)]


def on_device(physical, pair_slot, legendre, spectral_state, inverses, block_index):
    pair_count = pair_slot.shape[0]
    per_dev, _, degrees = legendre.shape
    starts, first = [], 0
    for n in CHUNKS:
        starts.append((first, n))
        first += n
    sends = list(prep(physical, pair_slot, tuple(starts), per_dev))

    lat, rad = lax.axis_index("lat"), lax.axis_index("rad")
    zl, y = rad // Y, rad % Y
    slots = lat * per_dev + jnp.arange(per_dev, dtype=jnp.int32)
    matches = pair_slot[None, :] == slots[:, None]
    owners = jnp.sum(jnp.where(matches, jnp.arange(pair_count, dtype=jnp.int32), 0), axis=1)
    stride = degrees // 2 // pair_count
    lengths = degrees - (1 + owners * stride)
    hops = jnp.arange(8, dtype=jnp.int32)
    blocks = (zl ^ (hops // Y)) * Y + (y + hops) % Y
    place = jnp.stack([zl, y]).astype(jnp.int32)

    out, gots, moves = None, [], []

    final = len(starts) - 1

    def put(k):
        return settle(
            moves[k],
            spectral_state,
            inverses,
            block_index,
            place,
            *starts[k],
            FLIPPED[k],
            out,
        )

    for k in range(len(starts) + 1):
        keep = {}
        if k > 0:
            keep["got", k - 1] = gots[k - 1]
        for chunk, hops_of in TIES.get(k, ()):
            for h in hops_of:
                keep["move", chunk, h] = moves[chunk][h]
        if k > 2:
            keep["out"] = out
        if k < len(starts):
            keep["send", k] = sends[k]
        held = dict(zip(keep, lax.optimization_barrier(tuple(keep.values()))))
        out = held.get("out", out)
        if k > 0:
            gots[k - 1] = held["got", k - 1]
        for name, value in held.items():
            if name[0] == "move":
                moves[name[1]][name[2]] = value
        if k < len(starts):
            send = held["send", k]
            if FLIPPED[k]:
                gots.append(
                    lax.all_to_all(
                        send, ("rad", "lat"), 0, 0, tiled=True, axis_index_groups=flip_groups()
                    )
                )
            else:
                gots.append(lax.all_to_all(send, "lat", 0, 0, tiled=True))
        if k > 0:
            first, n = starts[k - 1]
            meta = jnp.concatenate([(lat // 8)[None], blocks, lengths[first : first + n]])
            meta = meta.astype(jnp.int32)
            by_hop = True
            parts = transform(gots[k - 1], legendre, meta, first, FLIPPED[k - 1], by_hop)
            if by_hop:
                moved = {0: parts[0]}
                for h in ORDER:
                    moved[h] = lax.ppermute(parts[h], "rad", rad_targets(h // Y, h % Y))
                moves.append([moved[h] for h in range(8)])
            else:
                moves.append([lax.all_to_all(parts, "rad", 0, 0, tiled=True)])
        if k > 1:
            out = put(k - 2)
    return put(final)


def solution(mesh):
    in_specs = (
        P(None, None, "rad", "lat"),
        P(),
        P("lat", None, None),
        P("lat", None, None, "rad"),
        P(),
        P("lat", "rad"),
    )
    out_specs = P("lat", None, None, "rad")
    return jax.shard_map(
        on_device, mesh=mesh, in_specs=in_specs, out_specs=out_specs, check_vma=False
    )
```

```python
import functools

import jax
import jax.numpy as jnp
from jax import lax
from jax.experimental import pallas as pl
from jax.experimental.pallas import tpu as pltpu
from jax.sharding import PartitionSpec as P

ZS, Y = 2, 4
CHUNKS = (4, 2, 2)
FLIPPED = (False, True, True)
TIES = {2: ((0, (0, 1, 2, 3, 4, 5, 7)),), 3: ((0, (6,)), (1, (0, 1, 2, 3, 5, 6, 7)))}
ORDER = (6, 2, 5, 7, 1, 3, 4)
STEP = 16
BF16, F32 = jnp.bfloat16, jnp.float32


def prep_kernel(starts, per_dev, key_ref, x_ref, *refs):
    outs, (pick, swap, by_lat, by_order) = refs[: len(starts)], refs[len(starts) :]
    rows, _, orders = x_ref.shape

    @pl.when(pl.program_id(0) == 0)
    def _():
        at = 0
        for first, n in starts:
            count = 16 * n * 2
            i = lax.broadcasted_iota(jnp.int32, (count, orders), 0)
            rest, dest = i // 16, i % 16
            target = dest * (2 * per_dev) + 2 * first + rest
            hit = key_ref[...] == target
            pick[at : at + count, :] = jnp.where(hit, 1.0, 0.0).astype(BF16)
            at += count
        i = lax.broadcasted_iota(jnp.int32, (256, 256), 0)
        j = lax.broadcasted_iota(jnp.int32, (256, 256), 1)
        hit = (i // 16 == j % 16) & (i % 16 == j // 16)
        swap[...] = jnp.where(hit, 1.0, 0.0).astype(BF16)

    def to_lat(c, carry):
        at = pl.multiple_of(c * 16, 16)
        block = x_ref[pl.ds(at, 16), :, :].reshape(256, orders)
        moved = jnp.dot(swap[...], block, preferred_element_type=F32)
        by_lat[:, pl.ds(at, 16), :] = moved.astype(BF16).reshape(STEP, 16, orders)
        return carry

    lax.fori_loop(0, rows // 16, to_lat, 0, unroll=True)

    def to_order(n, carry):
        moved = lax.dot_general(
            pick[...], by_lat[n], (((1,), (1,)), ((), ())), preferred_element_type=F32
        )
        by_order[:, n] = moved.astype(BF16).reshape(by_order.shape[0], 16, rows)
        return carry

    lax.fori_loop(0, STEP, to_order, 0, unroll=True)

    base = 0
    for out, (_, n) in zip(outs, starts):
        for g in range(2 * n):
            block = by_order[base + g].reshape(256, rows)
            moved = jnp.dot(swap[...], block, preferred_element_type=F32).astype(BF16)
            out[:, g // 2, g % 2] = moved.reshape(16, STEP, rows)
        base += 2 * n


def prep(physical, pair_slot, starts, per_dev):
    orders, chans, radii, lats = physical.shape
    sent = sum(32 * n for _, n in starts)
    rows = chans * radii
    x = jnp.transpose(physical, (1, 2, 3, 0)).reshape(rows, lats, orders)
    key = (2 * pair_slot[:, None] + jnp.arange(2, dtype=jnp.int32)[None, :]).reshape(1, orders)
    return pl.pallas_call(
        functools.partial(prep_kernel, starts, per_dev),
        grid=(lats // STEP,),
        in_specs=[
            pl.BlockSpec((1, orders), lambda b: (0, 0)),
            pl.BlockSpec((rows, STEP, orders), lambda b: (0, b, 0)),
        ],
        out_specs=[
            pl.BlockSpec((16, n, 2, STEP, rows), lambda b: (0, 0, 0, b, 0)) for _, n in starts
        ],
        out_shape=[pltpu.HBM((16, n, 2, lats, rows), BF16) for _, n in starts],
        scratch_shapes=[
            pltpu.VMEM((sent, orders), BF16),
            pltpu.VMEM((256, 256), BF16),
            pltpu.VMEM((STEP, rows, orders), BF16),
            pltpu.VMEM((sent // 16, STEP, 16, rows), BF16),
        ],
        compiler_params=pltpu.CompilerParams(vmem_limit_bytes=48 << 20),
        cost_estimate=pl.CostEstimate(
            flops=2 * rows * lats * orders * (orders + 2 * sent),
            bytes_accessed=2 * rows * lats * (orders + sent),
            transcendentals=0,
        ),
        name="prep",
    )(key, x)


def spread(full, row, meta_ref, outs):
    for k in range(8):
        if len(outs) == 8:
            at = pl.multiple_of(meta_ref[1 + k] * 128, 128)
            outs[k][row] = full[:, pl.ds(at, 128)]
        else:
            outs[0][(k, *row)] = full[:, k * 128 : (k + 1) * 128]


def transform_kernel(meta_ref, got_ref, table_ref, *refs):
    outs, full = refs[:-1], refs[-1]
    slot = pl.program_id(0)
    half = table_ref.shape[2] // 2
    depth = table_ref.shape[1]
    rows = got_ref.shape[4]
    low_in = got_ref[:, 0, 0].reshape(depth, rows)
    high_in = got_ref[:, 0, 1].reshape(depth, rows)
    length = meta_ref[9 + slot]
    dims = (((0,), (0,)), ((), ()))
    low = lax.dot_general(low_in, table_ref[0], dims, preferred_element_type=F32)
    high = lax.dot_general(high_in, table_ref[0, :, half:], dims, preferred_element_type=F32)
    column = half + lax.broadcasted_iota(jnp.int32, high.shape, 1)
    full[:, :half] = low[:, :half].astype(BF16)
    full[:, half:] = jnp.where(column < length, low[:, half:], high).astype(BF16)
    spread(full, (0, 0), meta_ref, outs)


def transform_whole_kernel(meta_ref, got_ref, table_ref, *refs):
    outs, full = refs[:-1], refs[-1]
    slot, part = pl.program_id(0), pl.program_id(1)
    srcs, _, _, lats, rows = got_ref.shape
    depth, width = srcs * lats, table_ref.shape[2]
    dims = (((0,), (0,)), ((), ()))

    def product(h):
        return lax.dot_general(
            got_ref[:, 0, h].reshape(depth, rows),
            table_ref[0],
            dims,
            preferred_element_type=F32,
        )

    @pl.when(part == 0)
    def _():
        full[:, :width] = product(0).astype(BF16)

    @pl.when(part == 1)
    def _():
        column = width + lax.broadcasted_iota(jnp.int32, (rows, width), 1)
        chosen = jnp.where(column < meta_ref[9 + slot], product(0), product(1))
        full[:, width:] = chosen.astype(BF16)
        spread(full, (0,), meta_ref, outs)


def transform(got, legendre, meta, first, flipped, by_hop):
    srcs, count, _, lats, rows = got.shape
    degrees = legendre.shape[2]
    if flipped:
        kernel = transform_kernel
        depth, width = srcs // 2 * lats, degrees
        got_spec = pl.BlockSpec(
            (srcs // 2, 1, 2, lats, rows), lambda s, t, m: (t ^ m[0], s, 0, 0, 0)
        )
        table_spec = pl.BlockSpec((1, depth, width), lambda s, t, m: (first + s, t ^ m[0], 0))
        shape, block = (2, count, rows, 128), (1, 1, rows, 128)
        where = lambda s, t, m: (t, s, 0, 0)
    else:
        kernel = transform_whole_kernel
        depth, width = srcs * lats, degrees // 2
        got_spec = pl.BlockSpec((srcs, 1, 2, lats, rows), lambda s, t, m: (0, s, 0, 0, 0))
        table_spec = pl.BlockSpec((1, depth, width), lambda s, t, m: (first + s, 0, t))
        shape, block = (count, rows, 128), (1, rows, 128)
        where = lambda s, t, m: (s, 0, 0)
    if by_hop:
        out_specs = [pl.BlockSpec(block, where)] * 8
        out_shape = [pltpu.HBM(shape, BF16)] * 8
    else:
        out_specs = pl.BlockSpec((8,) + block, lambda s, t, m: (0, *where(s, t, m)))
        out_shape = pltpu.HBM((8,) + shape, BF16)
    return pl.pallas_call(
        kernel,
        grid_spec=pltpu.PrefetchScalarGridSpec(
            num_scalar_prefetch=1,
            grid=(count, 2),
            in_specs=[got_spec, table_spec],
            out_specs=out_specs,
            scratch_shapes=[pltpu.VMEM((rows, degrees), BF16)],
        ),
        out_shape=out_shape,
        compiler_params=pltpu.CompilerParams(vmem_limit_bytes=48 << 20),
        cost_estimate=pl.CostEstimate(
            flops=3 * count * rows * srcs * lats * degrees,
            bytes_accessed=2 * count * srcs * lats * (2 * rows + degrees),
            transcendentals=0,
        ),
        name="transform",
    )(meta, pltpu.with_memory_space_constraint(got, pltpu.HBM), legendre)


def invert(row, inv_ref, out_ref, side):
    row = jnp.concatenate([row, row], axis=1)
    for q in range(4):
        every = inv_ref[q].reshape(4 * 256, 256)
        found = jnp.dot(every, side[q], preferred_element_type=F32)
        acc = found[:256]
        for g in range(1, 4):
            acc = jnp.where(row == g, found[g * 256 : (g + 1) * 256], acc)
        acc = acc.astype(BF16)
        out_ref[0, 2 * q] = acc[:, :128]
        out_ref[0, 2 * q + 1] = acc[:, 128:]


def settle_kernel(first, flipped, meta_ref, *refs):
    parts = refs[:-5]
    state_ref, index_ref, inv_ref, out_ref, side = refs[-5:]
    radii = 32

    def part(zs, ys, *where):
        if len(parts) == 8:
            return parts[zs * Y + ys][where].astype(F32)
        return parts[0][(zs * Y + ys, *where)].astype(F32)

    for zs in range(ZS):
        for ys in range(Y):
            at = (zs * Y + ys) * radii
            if len(parts) == 8:
                zl, y = meta_ref[0], meta_ref[1]
                at = pl.multiple_of(((zl ^ zs) * Y + lax.rem(y + (Y - ys), Y)) * radii, radii)
            for c in range(8):
                rows = slice(c * radii, (c + 1) * radii)
                if flipped:
                    total = part(zs, ys, 0, 0, rows) + part(1 - zs, ys, 1, 0, rows)
                else:
                    total = part(zs, ys, 0, rows)
                value = state_ref[0, c, pl.ds(at, radii), :].astype(F32) + 0.5 * total
                lanes = slice((c % 2) * 128, (c % 2) * 128 + 128)
                side[c // 2, pl.ds(at, radii), lanes] = value.astype(BF16)
    invert(index_ref[pl.ds(first + pl.program_id(0), 1), :], inv_ref, out_ref, side)


def settle_chained_kernel(first, flipped, meta_ref, *refs):
    settle_kernel(first, flipped, meta_ref, *refs[:-3], *refs[-2:])


def settle(parts, state, inverses, index, meta, first, count, flipped, so_far):
    shape = parts[0].shape
    block = [1 if i == len(shape) - 3 else n for i, n in enumerate(shape)]
    lead = (0,) * (len(shape) - 3)
    operands = [meta, *parts, state, index, inverses]
    in_specs = [pl.BlockSpec(block, lambda s, m: (*lead, s, 0, 0))] * len(parts) + [
        pl.BlockSpec((1,) + state.shape[1:], lambda s, m: (first + s, 0, 0, 0)),
        pl.BlockSpec(index.shape, lambda s, m: (0, 0)),
        pl.BlockSpec(inverses.shape, lambda s, m: (0, 0, 0, 0)),
    ]
    kernel = settle_kernel if so_far is None else settle_chained_kernel
    aliases = {}
    if so_far is not None:
        operands.append(so_far)
        in_specs.append(pl.BlockSpec(memory_space=pl.ANY))
        aliases = {len(operands) - 1: 0}
    return pl.pallas_call(
        functools.partial(kernel, first, flipped),
        grid_spec=pltpu.PrefetchScalarGridSpec(
            num_scalar_prefetch=1,
            grid=(count,),
            in_specs=in_specs,
            out_specs=pl.BlockSpec((1,) + state.shape[1:], lambda s, m: (first + s, 0, 0, 0)),
            scratch_shapes=[pltpu.VMEM((4, 256, 256), BF16)],
        ),
        out_shape=jax.ShapeDtypeStruct(state.shape, BF16),
        input_output_aliases=aliases,
        compiler_params=pltpu.CompilerParams(vmem_limit_bytes=48 << 20),
        cost_estimate=pl.CostEstimate(
            flops=2 * count * 16 * 256 * 256 * 256,
            bytes_accessed=count * (2 << 20) + (2 << 20),
            transcendentals=0,
        ),
        name="settle",
    )(*operands)


def flip_groups():
    groups = []
    for y in range(Y):
        for zl in range(ZS):
            groups.append([((zl ^ (l // 8)) * Y + y) * 16 + l for l in range(16)])
    return groups


def rad_targets(kz, ky):
    return [(i, ((i // Y) ^ kz) * Y + (i % Y + ky) % Y) for i in range(ZS * Y)]


def on_device(physical, pair_slot, legendre, spectral_state, inverses, block_index):
    pair_count = pair_slot.shape[0]
    per_dev, _, degrees = legendre.shape
    starts, first = [], 0
    for n in CHUNKS:
        starts.append((first, n))
        first += n
    sends = list(prep(physical, pair_slot, tuple(starts), per_dev))

    lat, rad = lax.axis_index("lat"), lax.axis_index("rad")
    zl, y = rad // Y, rad % Y
    slots = lat * per_dev + jnp.arange(per_dev, dtype=jnp.int32)
    matches = pair_slot[None, :] == slots[:, None]
    owners = jnp.sum(jnp.where(matches, jnp.arange(pair_count, dtype=jnp.int32), 0), axis=1)
    stride = degrees // 2 // pair_count
    lengths = degrees - (1 + owners * stride)
    hops = jnp.arange(8, dtype=jnp.int32)
    blocks = (zl ^ (hops // Y)) * Y + (y + hops) % Y
    place = jnp.stack([zl, y]).astype(jnp.int32)

    out, gots, moves = None, [], []

    final = len(starts) - 1

    def put(k):
        return settle(
            moves[k],
            spectral_state,
            inverses,
            block_index,
            place,
            *starts[k],
            FLIPPED[k],
            out,
        )

    for k in range(len(starts) + 1):
        keep = {}
        if k > 0:
            keep["got", k - 1] = gots[k - 1]
        for chunk, hops_of in TIES.get(k, ()):
            for h in hops_of:
                keep["move", chunk, h] = moves[chunk][h]
        if k > 2:
            keep["out"] = out
        if k < len(starts):
            keep["send", k] = sends[k]
        held = dict(zip(keep, lax.optimization_barrier(tuple(keep.values()))))
        out = held.get("out", out)
        if k > 0:
            gots[k - 1] = held["got", k - 1]
        for name, value in held.items():
            if name[0] == "move":
                moves[name[1]][name[2]] = value
        if k < len(starts):
            send = held["send", k]
            if FLIPPED[k]:
                gots.append(
                    lax.all_to_all(
                        send, ("rad", "lat"), 0, 0, tiled=True, axis_index_groups=flip_groups()
                    )
                )
            else:
                gots.append(lax.all_to_all(send, "lat", 0, 0, tiled=True))
        if k > 0:
            first, n = starts[k - 1]
            meta = jnp.concatenate([(lat // 8)[None], blocks, lengths[first : first + n]])
            meta = meta.astype(jnp.int32)
            by_hop = True
            parts = transform(gots[k - 1], legendre, meta, first, FLIPPED[k - 1], by_hop)
            if by_hop:
                moved = {0: parts[0]}
                for h in ORDER:
                    moved[h] = lax.ppermute(parts[h], "rad", rad_targets(h // Y, h % Y))
                moves.append([moved[h] for h in range(8)])
            else:
                moves.append([lax.all_to_all(parts, "rad", 0, 0, tiled=True)])
        if k > 1:
            out = put(k - 2)
    return put(final)


def solution(mesh):
    in_specs = (
        P(None, None, "rad", "lat"),
        P(),
        P("lat", None, None),
        P("lat", None, None, "rad"),
        P(),
        P("lat", "rad"),
    )
    out_specs = P("lat", None, None, "rad")
    return jax.shard_map(
        on_device, mesh=mesh, in_specs=in_specs, out_specs=out_specs, check_vma=False
    )
```
